32 devices in a mesh: grp: 2 (over core), pen: 4 (over z), blk: 4 (over y, x).
Axes of the slice: x: 2, y: 2, z: 4, core: 2. Of those that a mesh axis runs over, the one named last changes fastest.
Arguments:
- tile_blocks: bfloat16 [1024, 128, 128], P(('grp', 'pen', 'blk')), may hold values from -0.19921875 to 0.19921875
- tile_aux: int32 [1024], P(('grp', 'pen', 'blk')), may hold values from 0 to 31, as said below
- tile_pair: int32 [1024], P(('grp', 'pen', 'blk')), may hold values from 0 to 127
- tile_count: int32 [32], P(('grp', 'pen', 'blk')), may hold values from 4 to 32, as said below
- density: bfloat16 [128, 128], P('blk'), may hold values from -6 to 6
- metric_inv: float32 [32, 128, 128], P('pen'), may hold values from -0.5 to 0.5
- orbitals: bfloat16 [8, 192, 36864], P(None, 'pen'), may hold values from -6 to 6
- pair_index: int32 [16, 2], P(('grp', 'blk')), may hold values from 0 to 7, as said below
Outputs:
- coulomb: float32 [128, 128], P(('grp', 'pen', 'blk'))
- pair_terms: float32 [16, 192, 36864], P(('grp', 'blk'), 'pen')
The draws below stay inside these ranges and needn't reach their ends.
Inputs may be any that keep to these rules, and one draw needn't show every extreme that they name: `tile_aux`: the auxiliary block of a slot is one of the 8 blocks a * 8 to a * 8 + 7 where a is the pen index of the device holding the slot (slots laid out over grp, pen, blk, slowest first, 32 a device); padding slots hold such indices too. Device d uses the first tile_count[d] of its 32 slots; the rest is padding with arbitrary contents; some device uses all 32 slots. `pair_index`: each row names two different orbitals.
All inputs are finite; a program needn't handle non-finite values.
Results may differ from the reference program's by a relative error of at most 0.0029.
Values may be sent and summed in bfloat16 or wider, within the bound.
No kernel may reach another device: no remote copies, remote signals or barrier semaphores. Data moves between devices by JAX's collectives and lax.ppermute only.
A program may use at most 320 MiB of HBM per device.

```python
import math
import jax
import jax.numpy as jnp
from jax import lax

AB = 128
PB = 128
AUX_DEV = 8
TMAX = 32
NG = 192
NORB = 8
NDEV = 32
TSLOTS = 1024
NPB = 128
NAB = 32
NPAIR = 16
N_PEN = 4
N_BLK = 4


def draw_tile_aux(key, part):
    key = jax.random.fold_in(key, 3)
    slot_ids = jnp.arange(TMAX * NDEV, dtype=jnp.int32)
    owner = slot_ids // TMAX // N_BLK % N_PEN
    offset = jax.random.randint(key, (TMAX * NDEV,), 0, AUX_DEV, dtype=jnp.int32)
    return owner * AUX_DEV + offset


def draw_tile_count(key, part):
    key = jax.random.fold_in(key, 5)
    keys = jax.random.split(key, 5)
    light = jax.random.randint(keys[0], (NDEV,), TMAX // 8, TMAX // 2 + 1, dtype=jnp.int32)
    heavy = TMAX - jax.random.randint(keys[1], (NDEV,), 0, TMAX // 8 + 1, dtype=jnp.int32)
    busy = jax.random.randint(keys[2], (NDEV,), 0, 4, dtype=jnp.int32) == 0
    counts = jnp.where(busy, heavy, light)
    device_ids = jnp.arange(NDEV, dtype=jnp.int32)
    fullest = jax.random.randint(keys[3], (), 0, NDEV, dtype=jnp.int32)
    lightest = (fullest + 1 + jax.random.randint(keys[4], (), 0, NDEV - 1, dtype=jnp.int32)) % NDEV
    counts = jnp.where(device_ids == lightest, TMAX // 8, counts)
    counts = jnp.where(device_ids == fullest, TMAX, counts)
    return counts.astype(jnp.int32)


def draw_pair_index(key, part):
    key = jax.random.fold_in(key, 7)
    keys = jax.random.split(key, 2)
    first_orbital = jax.random.randint(keys[0], (NPAIR,), 0, NORB, dtype=jnp.int32)
    offset = jax.random.randint(keys[1], (NPAIR,), 1, NORB, dtype=jnp.int32)
    second_orbital = (first_orbital + offset) % NORB
    return jnp.stack([first_orbital, second_orbital], axis=1).astype(jnp.int32)


def set_ends(values, stream_key, least, top_value):
    spot = [jax.random.randint(jax.random.fold_in(stream_key, axis), (), 0, length) for axis, length in enumerate(values.shape)]
    widest = values.shape.index(max(values.shape))
    beside = spot[:widest] + [(spot[widest] + 1) % values.shape[widest]] + spot[widest + 1:]
    return values.at[tuple(spot)].set(least).at[tuple(beside)].set(top_value)


def level_of(stream_key, extent, cuts, low, high):
    gain = 1.0
    for axis_at, parts in cuts:
        heights = jax.random.uniform(jax.random.fold_in(jax.random.fold_in(stream_key, 6), axis_at), (parts,), jnp.float32, low / len(cuts), high / len(cuts))
        gain = gain * jnp.repeat(jnp.exp(heights), extent[axis_at] // parts).reshape((-1,) + (1,) * (len(extent) - 1 - axis_at))
    return gain


def scatter_about(rng, extent, width, reach, cuts=(), kind=jnp.bfloat16):
    drawn = jax.random.normal(rng, extent, jnp.float32) * width
    if len(cuts) > 0:
        drawn = level_of(rng, extent, cuts, -0.22, 0.18) * drawn
    return jnp.clip(drawn, min=-reach, max=reach).astype(kind)


def setup_inputs(seed: int = 0) -> dict:
    arg_keys = jax.random.split(jax.random.key(seed), 9)
    tile_blocks = scatter_about(arg_keys[0], (TSLOTS, AB, PB), 0.03, 0.19921875, ((0, 32),))
    tile_aux = draw_tile_aux(jax.random.fold_in(arg_keys[8], 71), 0)
    tile_pair = set_ends(jax.random.randint(arg_keys[2], (TSLOTS,), 0, NPB), jax.random.fold_in(arg_keys[2], 1), 0, NPB - 1).astype(jnp.int32)
    tile_count = draw_tile_count(jax.random.fold_in(arg_keys[8], 71), 0)
    density = scatter_about(arg_keys[4], (NPB, PB), 1.0, 6.0, ((0, 4),))
    metric_inv = scatter_about(arg_keys[5], (NAB, AB, AB), AB ** -0.5, 0.5, ((0, 4),), jnp.float32)
    orbitals = scatter_about(arg_keys[6], (NORB, NG, NG * NG), 1.0, 6.0, ((1, 4),))
    pair_index = draw_pair_index(jax.random.fold_in(arg_keys[8], 71), 0)
    return {"tile_blocks": tile_blocks, "tile_aux": tile_aux, "tile_pair": tile_pair, "tile_count": tile_count, "density": density, "metric_inv": metric_inv, "orbitals": orbitals, "pair_index": pair_index}


PRECISE = lax.Precision.HIGHEST
SPACING = 0.1348

def signed_freq(position, length):
    return jnp.where(position < length // 2, position, position - length)

def coulomb_kernel(square_sum, length):
    box_length = SPACING * length
    kernel_scale = box_length * box_length / math.pi
    squares = square_sum.astype(jnp.float32)
    magnitude = jnp.sqrt(squares)
    denominator = jnp.where(square_sum == 0, 1.0, squares)
    regular = kernel_scale * (1.0 - jnp.cos(math.pi * magnitude)) / denominator
    return jnp.where(square_sum == 0, kernel_scale * math.pi * math.pi / 2.0, regular).astype(jnp.float32)

def reference(tile_blocks, tile_aux, tile_pair, tile_count, density, metric_inv, orbitals, pair_index):
    slot_ids = jnp.arange(NDEV * TMAX, dtype=jnp.int32)
    live_slots = (slot_ids % TMAX < jnp.repeat(tile_count, TMAX)).astype(jnp.float32)
    grouped = (tile_blocks.reshape(NDEV, TMAX, AB, PB), tile_aux.reshape(NDEV, TMAX), tile_pair.reshape(NDEV, TMAX), live_slots.reshape(NDEV, TMAX))

    def fit_step(gamma, group):
        blocks_in, aux_in, pair_in, weights_in = group
        dens_rows = density[pair_in].astype(jnp.float32)
        partial_value = jnp.einsum('tap,tp->ta', blocks_in.astype(jnp.float32), dens_rows, precision=PRECISE)
        partial_value = partial_value * weights_in[:, None]
        return (gamma.at[aux_in].add(partial_value), None)
    gamma = lax.scan(fit_step, jnp.zeros((NAB, AB), jnp.float32), grouped)[0]
    coef = jnp.einsum('kab,kb->ka', metric_inv, gamma, precision=PRECISE).astype(jnp.bfloat16)

    def build_step(running, group):
        blocks_in, aux_in, pair_in, weights_in = group
        coef_rows = coef[aux_in].astype(jnp.float32)
        partial_value = jnp.einsum('tap,ta->tp', blocks_in.astype(jnp.float32), coef_rows, precision=PRECISE)
        partial_value = partial_value * weights_in[:, None]
        return (running.at[pair_in].add(partial_value), None)
    coulomb = lax.scan(build_step, jnp.zeros((NPB, PB), jnp.float32), grouped)[0]
    grid_ids = signed_freq(jnp.arange(NG, dtype=jnp.int32), NG)
    square_sum = grid_ids[:, None, None] * grid_ids[:, None, None] + grid_ids[None, :, None] * grid_ids[None, :, None] + grid_ids[None, None, :] * grid_ids[None, None, :]
    kernel_grid = coulomb_kernel(square_sum, NG)
    orbital_grid = orbitals.reshape(NORB, NG, NG, NG)

    def pair_field(pair_row):
        left_orbital = orbital_grid[pair_row[0]].astype(jnp.float32)
        right_orbital = orbital_grid[pair_row[1]].astype(jnp.float32)
        pair_density = left_orbital * right_orbital
        potential = jnp.real(jnp.fft.ifftn(jnp.fft.fftn(pair_density) * kernel_grid)).astype(jnp.float32)
        return (potential * right_orbital).reshape(NG, NG * NG)
    pair_terms = lax.map(pair_field, pair_index)
    return (coulomb, pair_terms)
```

```python
import functools
import math

import jax
import jax.numpy as jnp
import ml_dtypes
import numpy as np
from jax import lax
from jax.experimental import pallas as pl
from jax.experimental.pallas import tpu as pltpu
from jax.sharding import PartitionSpec as P

NG = 192
LANE = 128
TAIL = NG - LANE
PAIR_LANES = 2 * NG
ROWS = 16
NEAR = 2

PRECISE = lax.Precision.HIGHEST
SPACING = 0.1348
VMEM_BYTES = 56 * 1024 * 1024


def signed_freq(position, length):
    return jnp.where(position < length // 2, position, position - length)


def coulomb_kernel(square_sum, length):
    box_length = SPACING * length
    kernel_scale = box_length * box_length / math.pi
    squares = square_sum.astype(jnp.float32)
    magnitude = jnp.sqrt(squares)
    denominator = jnp.where(square_sum == 0, 1.0, squares)
    regular = kernel_scale * (1.0 - jnp.cos(math.pi * magnitude)) / denominator
    return jnp.where(square_sum == 0, kernel_scale * math.pi * math.pi / 2.0, regular)


def cas_table(left, right):
    angles = (left * right % NG) * (2.0 * math.pi / NG)
    return np.cos(angles) + np.sin(angles)


def split_table(table):
    high = table.astype(ml_dtypes.bfloat16)
    return high, (table - high.astype(np.float64)).astype(ml_dtypes.bfloat16)


def split(values):
    high = values.astype(jnp.bfloat16)
    low = (values - high.astype(jnp.float32)).astype(jnp.bfloat16)
    return high, low


def split_rest(values):
    high = values.astype(jnp.bfloat16).astype(jnp.float32)
    return high, values - high


def width_of(slab):
    return slab * NG


def dot32(left, right):
    return jnp.dot(left, right, preferred_element_type=jnp.float32)


def split_dot(values, high_weight, low_weight):
    high, low = split(values)
    return dot32(high, high_weight) + dot32(high, low_weight) + dot32(low, high_weight)


def stacked_dot(stacked, values):
    count = stacked.shape[0] // 2
    high, low = split(values)
    both = dot32(stacked, high)
    return both[:count] + both[count:] + dot32(stacked[:count], low)


def stacked_dot_exact(stacked, values):
    count = stacked.shape[0] // 2
    both = dot32(stacked, values)
    return both[:count] + both[count:]


def forward_kernel(slab, pen, meta_ref, left_ref, right_ref, depth_ref, cols_ref, *refs):
    outs, (rows_ref, head_ref, tail_ref, rest_ref) = refs[-4 - pen : -4], refs[-4:]
    half = NG // 2
    chunk = 32

    def depth_step(step, carry):
        start = pl.multiple_of(step * (chunk * PAIR_LANES), LANE)
        lanes = pl.ds(start, chunk * PAIR_LANES)
        field = left_ref[0, :, lanes].astype(jnp.float32) * right_ref[0, :, lanes].astype(jnp.float32)
        high, low = split(field)
        for parity in range(2):
            parts = []
            for source in (high, low):
                first = parity * LANE
                parts.append(
                    jnp.concatenate(
                        [source[:, k * PAIR_LANES + first : k * PAIR_LANES + first + 2 * LANE] for k in range(chunk)], axis=0
                    )
                )
            table_high, table_low = depth_ref[parity, 0], depth_ref[parity, 1]
            result = dot32(parts[0], table_high) + dot32(parts[0], table_low) + dot32(parts[1], table_high)
            place = pl.ds(pl.multiple_of((parity * half + step * chunk) * ROWS, ROWS), chunk * ROWS)
            rows_ref[0, place, :] = result[:, :LANE]
            rows_ref[1, place, :] = result[:, LANE:]
        return carry

    lax.fori_loop(0, half // chunk, depth_step, 0)
    low_lanes = lax.broadcasted_iota(jnp.int32, (slab // 2, LANE), 1) < TAIL

    @pl.when(pl.program_id(0) == 0)
    def _():
        rest_ref[...] = jnp.zeros_like(rest_ref)

    def rounded(values, place):
        values = values + rest_ref[place, :]
        kept = values.astype(jnp.bfloat16).astype(jnp.float32)
        rest_ref[place, :] = values - kept
        return kept

    def cols_step(plane, carry):
        strided = pl.ds(plane, NG, stride=ROWS)
        field = jnp.concatenate([rows_ref[0, strided, :], rows_ref[1, strided, :]], axis=1)
        result = stacked_dot(cols_ref[...], field)
        head_ref[strided, :] = rounded(result[:, :LANE], pl.ds(0, NG))
        tails = []
        for q in range(pen):
            first = result[q * slab : q * slab + slab // 2, LANE:]
            second = result[q * slab + slab // 2 : (q + 1) * slab, LANE:]
            tails.append(jnp.where(low_lanes, first, second))
        tail_ref[pl.ds(plane, half, stride=ROWS), :] = rounded(jnp.concatenate(tails, axis=0), pl.ds(NG, half))
        return carry

    lax.fori_loop(0, ROWS, cols_step, 0, unroll=4)
    for s in range(pen):
        owner = meta_ref[2] ^ s
        for r in range(slab):
            place = pl.ds(pl.multiple_of((owner * slab + r) * ROWS, ROWS), ROWS)
            outs[s][:, r * LANE : (r + 1) * LANE] = head_ref[place, :].astype(jnp.bfloat16)
        for r in range(slab // 2):
            place = pl.ds(pl.multiple_of((owner * (slab // 2) + r) * ROWS, ROWS), ROWS)
            outs[s][:, (slab + r) * LANE : (slab + r + 1) * LANE] = tail_ref[place, :].astype(jnp.bfloat16)


def middle_kernel(pen, in_pieces, out_pieces, extra, meta_ref, table_ref, grid_ref, part_ref, *refs):
    fields, outs, planes_ref = refs[: len(in_pieces)], refs[len(in_pieces) : -1], refs[-1]
    slab = NG // pen
    block = planes_ref.shape[1]

    def place(s, first, count):
        return pl.ds(pl.multiple_of((meta_ref[2] ^ s) * slab + first, ROWS), count)

    for field, piece in zip(fields, in_pieces):
        planes_ref[place(*piece), :] = field[...]
    spectral = stacked_dot_exact(table_ref[...], planes_ref[...]) * grid_ref[...]
    planes_ref[...] = stacked_dot(table_ref[...], spectral).astype(jnp.bfloat16)
    for out_ref, piece in zip(outs, out_pieces):
        values = planes_ref[place(*piece), :]
        if not (extra and piece[1] + piece[2] == slab):
            out_ref[...] = values
            continue
        lanes = pl.ds(pl.multiple_of(pl.program_id(0) * block, LANE), block)
        out_ref[:, lanes] = values
        high, rest = split_rest(part_ref[meta_ref[2] ^ piece[0]])
        middle, rest = split_rest(rest)
        blank = jnp.zeros((ROWS - 3 * high.shape[0], LANE), jnp.float32)
        if piece[2] > ROWS:
            out_ref[: piece[2] - ROWS, width_of(slab) :] = jnp.zeros((piece[2] - ROWS, LANE), jnp.bfloat16)
        tag = jnp.concatenate([high, middle, rest, blank], axis=0).astype(jnp.bfloat16)
        out_ref[piece[2] - ROWS :, width_of(slab) :] = tag


def inverse_kernel(slab, pen, extra, meta_ref, *refs):
    fields = refs[:pen]
    right_ref, cols_ref, depth_ref = refs[pen : pen + 3]
    out_ref, rows_ref, head_ref, tail_ref = refs[-4:]
    if extra:
        part_ref, out_ref = refs[-4], refs[-5]
        rows = part_ref.shape[0]
        tags = [field[:, width_of(slab) :].astype(jnp.float32) for field in fields]
        part_ref[...] = sum(tag[c * rows : (c + 1) * rows] for c in (2, 1, 0) for tag in tags)
    half = NG // 2
    chunk = 32
    for s in range(pen):
        owner = meta_ref[2] ^ s
        for r in range(slab):
            place = pl.ds(pl.multiple_of((owner * slab + r) * ROWS, ROWS), ROWS)
            head_ref[place, :] = fields[s][:, r * LANE : (r + 1) * LANE].astype(jnp.float32)
        for r in range(slab // 2):
            place = pl.ds(pl.multiple_of((owner * (slab // 2) + r) * ROWS, ROWS), ROWS)
            tail_ref[place, :] = fields[s][:, (slab + r) * LANE : (slab + r + 1) * LANE].astype(jnp.float32)
    low_lanes = lax.broadcasted_iota(jnp.int32, (slab // 2, LANE), 1) < TAIL

    def cols_step(plane, carry):
        strided = pl.ds(plane, NG, stride=ROWS)
        tail = tail_ref[pl.ds(plane, half, stride=ROWS), :]
        pieces = []
        for q in range(pen):
            both = tail[q * (slab // 2) : (q + 1) * (slab // 2)]
            pieces.append(jnp.where(low_lanes, both, 0.0))
            pieces.append(jnp.where(low_lanes, 0.0, both))
        field = jnp.concatenate([head_ref[strided, :], jnp.concatenate(pieces, axis=0)], axis=1)
        result = stacked_dot_exact(cols_ref[...], field.astype(jnp.bfloat16))
        rows_ref[0, strided, :] = result[:, :LANE]
        rows_ref[1, strided, :] = result[:, LANE:]
        return carry

    lax.fori_loop(0, ROWS, cols_step, 0, unroll=4)

    def depth_step(step, carry):
        results = []
        for parity in range(2):
            place = pl.ds(pl.multiple_of((parity * half + step * chunk) * ROWS, ROWS), chunk * ROWS)
            field = jnp.concatenate([rows_ref[0, place, :], rows_ref[1, place, :]], axis=1)
            results.append(split_dot(field, depth_ref[parity, 0], depth_ref[parity, 1]))
        for k in range(chunk):
            even, odd = (value[k * ROWS : (k + 1) * ROWS] for value in results)
            potential = jnp.concatenate([even[:, :LANE], even[:, LANE:] + odd[:, :LANE], odd[:, LANE:]], axis=1)
            lanes = pl.ds(pl.multiple_of((step * chunk + k) * PAIR_LANES, LANE), PAIR_LANES)
            out_ref[0, :, lanes] = potential * right_ref[0, :, lanes].astype(jnp.float32)
        return carry

    lax.fori_loop(0, half // chunk, depth_step, 0)


def whole_spec(shape):
    return pl.BlockSpec(shape, lambda *_: (0,) * len(shape))


def column_scratch():
    return [
        pltpu.VMEM((2, NG * ROWS, LANE), jnp.float32),
        pltpu.VMEM((NG * ROWS, LANE), jnp.float32),
        pltpu.VMEM((NG // 2 * ROWS, LANE), jnp.float32),
    ]


def forward_planes(meta, orbitals, depth_tables, cols_table, pen, first, count, earlier, after):
    slab = NG // pen
    width = width_of(slab)
    skip = first // ROWS
    near = jax.ShapeDtypeStruct((slab, width), jnp.bfloat16)
    far = jax.ShapeDtypeStruct((count, width), jnp.bfloat16)
    operands = [meta, orbitals, orbitals, depth_tables, cols_table]
    aliases = {len(operands) + s: s for s in range(len(earlier))}
    operands += [*earlier, *after]
    return pl.pallas_call(
        functools.partial(forward_kernel, slab, pen),
        out_shape=[near] * NEAR + [far] * (pen - NEAR),
        grid_spec=pltpu.PrefetchScalarGridSpec(
            num_scalar_prefetch=1,
            grid=(count // ROWS,),
            in_specs=[
                pl.BlockSpec((1, ROWS, NG * NG), lambda b, meta: (meta[0], b + skip, 0)),
                pl.BlockSpec((1, ROWS, NG * NG), lambda b, meta: (meta[1], b + skip, 0)),
                whole_spec(depth_tables.shape),
                whole_spec(cols_table.shape),
            ]
            + [pl.BlockSpec(memory_space=pl.ANY)] * (len(earlier) + len(after)),
            out_specs=[pl.BlockSpec((ROWS, width), lambda b, meta: (b + skip, 0))] * NEAR
            + [pl.BlockSpec((ROWS, width), lambda b, meta: (b, 0))] * (pen - NEAR),
            scratch_shapes=column_scratch() + [pltpu.VMEM((NG + NG // 2, LANE), jnp.float32)],
        ),
        input_output_aliases=aliases,
        compiler_params=pltpu.CompilerParams(vmem_limit_bytes=VMEM_BYTES),
        cost_estimate=pl.CostEstimate(
            flops=2 * 6 * count * NG * NG * NG, bytes_accessed=6 * count * NG * NG, transcendentals=0
        ),
        name="forward_planes",
    )(*operands)


def middle_columns(meta, fields, in_pieces, table, grid_table, part, pen, out_pieces, extra):
    slab = NG // pen
    width = width_of(slab)
    block = width // 8
    out_shapes, out_specs = [], []
    for s, first, count in out_pieces:
        if extra and first + count == slab:
            out_shapes.append(jax.ShapeDtypeStruct((count, width + LANE), jnp.bfloat16))
            out_specs.append(whole_spec((count, width + LANE)))
        else:
            out_shapes.append(jax.ShapeDtypeStruct((count, width), jnp.bfloat16))
            out_specs.append(pl.BlockSpec((count, block), lambda b, meta: (0, b)))
    in_specs = [whole_spec(table.shape), pl.BlockSpec((NG, block), lambda b, meta: (0, b)), whole_spec(part.shape)]
    in_specs += [pl.BlockSpec((count, block), lambda b, meta: (0, b)) for s, first, count in in_pieces]
    return pl.pallas_call(
        functools.partial(middle_kernel, pen, in_pieces, out_pieces, extra),
        out_shape=out_shapes,
        grid_spec=pltpu.PrefetchScalarGridSpec(
            num_scalar_prefetch=1,
            grid=(width // block,),
            in_specs=in_specs,
            out_specs=out_specs,
            scratch_shapes=[pltpu.VMEM((NG, block), jnp.bfloat16)],
        ),
        compiler_params=pltpu.CompilerParams(vmem_limit_bytes=VMEM_BYTES),
        cost_estimate=pl.CostEstimate(flops=2 * 5 * NG * NG * width, bytes_accessed=8 * NG * width, transcendentals=0),
        name="middle_columns",
    )(meta, table, grid_table, part, *fields)


def inverse_planes(meta, fields, orbitals, cols_table, depth_tables, pair, pairs, first, earlier, part_rows):
    pen = len(fields)
    slab = NG // pen
    count = fields[-1].shape[0]
    skip = first // ROWS
    out_shapes = [jax.ShapeDtypeStruct((pairs, slab, NG * NG), jnp.float32)]
    out_specs = [pl.BlockSpec((1, ROWS, NG * NG), lambda b, meta: (pair, b + skip, 0))]
    if part_rows:
        out_shapes.append(jax.ShapeDtypeStruct((part_rows, LANE), jnp.float32))
        out_specs.append(whole_spec((part_rows, LANE)))
    in_specs = [pl.BlockSpec((ROWS, field.shape[1]), lambda b, meta: (b + skip, 0)) for field in fields[:NEAR]]
    in_specs += [pl.BlockSpec((ROWS, field.shape[1]), lambda b, meta: (b, 0)) for field in fields[NEAR:]]
    in_specs += [
        pl.BlockSpec((1, ROWS, NG * NG), lambda b, meta: (meta[1], b + skip, 0)),
        whole_spec(cols_table.shape),
        whole_spec(depth_tables.shape),
    ]
    operands = [meta, *fields, orbitals, cols_table, depth_tables]
    aliases = {}
    if earlier is not None:
        aliases = {len(operands): 0}
        in_specs.append(pl.BlockSpec(memory_space=pl.ANY))
        operands.append(earlier)
    return pl.pallas_call(
        functools.partial(inverse_kernel, slab, pen, bool(part_rows)),
        out_shape=out_shapes,
        grid_spec=pltpu.PrefetchScalarGridSpec(
            num_scalar_prefetch=1,
            grid=(count // ROWS,),
            in_specs=in_specs,
            out_specs=out_specs,
            scratch_shapes=column_scratch(),
        ),
        input_output_aliases=aliases,
        compiler_params=pltpu.CompilerParams(vmem_limit_bytes=VMEM_BYTES),
        cost_estimate=pl.CostEstimate(
            flops=2 * 5 * count * NG * NG * NG, bytes_accessed=8 * count * NG * NG, transcendentals=0
        ),
        name="inverse_planes",
    )(*operands)


def exchange(s, field, pen):
    return lax.ppermute(field, "pen", [(i, i ^ s) for i in range(pen)]) if s else field


def stack_split(table):
    return np.concatenate(split_table(table), axis=0)


def depth_table_set():
    lanes = np.arange(2 * LANE)
    freq = np.where(lanes < NG, lanes, lanes - TAIL)
    tables = []
    for parity in range(2):
        depth = lanes - parity * TAIL
        inside = (depth >= 0) & (depth < NG)
        tables.append(np.where(inside[:, None], cas_table(depth[:, None], freq[None, :]), 0.0))
    return np.stack(split_table(np.stack(tables)), axis=1)


def grid_weights(me, slab):
    lane = jnp.arange(LANE, dtype=jnp.int32)[None, :]
    row = jnp.arange(slab, dtype=jnp.int32)[:, None]
    head_col, head_depth = jnp.broadcast_arrays(row, lane)
    tail_row = row[: slab // 2]
    tail_col = jnp.where(lane < TAIL, tail_row, tail_row + slab // 2)
    tail_depth = jnp.broadcast_to(LANE + lane % TAIL, tail_col.shape)
    col = signed_freq(me * slab + jnp.concatenate([head_col, tail_col], axis=0).reshape(-1), NG)
    depth = signed_freq(jnp.concatenate([head_depth, tail_depth], axis=0).reshape(-1), NG)
    plane = signed_freq(jnp.arange(NG, dtype=jnp.int32), NG)
    square_sum = (plane * plane)[:, None] + (col * col + depth * depth)[None, :]
    return coulomb_kernel(square_sum, NG) / float(NG * NG * NG)


def plane_runs(slab, first, last):
    if slab > ROWS and first:
        return ((0, ROWS), (ROWS, slab - ROWS))
    if slab > ROWS and last:
        return ((0, slab - ROWS), (slab - ROWS, ROWS))
    return ((0, slab),)


def pieces_of(pen, runs):
    far = tuple((s, first, count) for first, count in runs for s in range(pen - 1, NEAR - 1, -1))
    return far + tuple((s, 0, NG // pen) for s in range(NEAR - 1, -1, -1))


def both_parts(orbitals, pair_index, pen, coulomb_part):
    slab = NG // pen
    pairs = pair_index.shape[0]
    me = lax.axis_index("pen").astype(jnp.int32)
    positions = np.arange(NG)
    interleaved = np.concatenate([positions[0::2], positions[1::2]])
    depth_np = depth_table_set()
    depth_tables, depth_back = jnp.asarray(depth_np), jnp.asarray(np.swapaxes(depth_np, 2, 3))
    cols_forward = jnp.asarray(stack_split(cas_table(positions[:, None], interleaved[None, :])))
    cols_back = jnp.asarray(stack_split(cas_table(interleaved[:, None], positions[None, :])))
    plane_table = jnp.asarray(stack_split(cas_table(positions[:, None], positions[None, :])))
    metas = [jnp.concatenate([pair_index[p], me[None]]) for p in range(pairs)]

    held, after = [], []
    for p in range(pairs):
        runs = plane_runs(slab, p == 0, False)
        taken, made = {}, ()
        for first, count in runs:
            made = forward_planes(
                metas[p], orbitals, depth_tables, cols_forward, pen, first, count, made[:NEAR], after if first == 0 else ()
            )
            for s in range(NEAR, pen):
                taken[s, first] = exchange(s, made[s], pen)
        for s in range(NEAR):
            taken[s, 0] = exchange(s, made[s], pen)
        pieces = pieces_of(pen, runs)
        held.append((pieces, [taken[s, first] for s, first, count in pieces]))
        if p == 0:
            local, part_of = coulomb_part(made[-1])
            after = [local] + [taken[s, 0] for s in range(NEAR, pen) if len(runs) > 1]
    late_me, _ = lax.optimization_barrier((me, made[-1]))
    grid_table = grid_weights(late_me, slab)
    part = part_of(local)

    back = []
    for p in range(pairs):
        last = p == pairs - 1
        fed = part if last else jnp.zeros_like(part)
        runs = plane_runs(slab, False, last)
        pieces = pieces_of(pen, runs)
        filtered = middle_columns(metas[p], held[p][1], held[p][0], plane_table, grid_table, fed, pen, pieces, last)
        back.append((runs, {piece[:2]: exchange(piece[0], field, pen) for piece, field in zip(pieces, filtered)}))

    terms = None
    for p in range(pairs):
        runs, taken = back[p]
        for first, count in runs:
            final = p == pairs - 1 and first + count == slab
            fields = [taken[s, 0 if s < NEAR else first] for s in range(pen)]
            made = inverse_planes(
                metas[p], fields, orbitals, cols_back, depth_back, p, pairs, first, terms, part.shape[1] if final else 0
            )
            terms = made[0]
    return made[1], terms


def pair_fields_plain(orbitals, pair_index, pen):
    slab = NG // pen
    plane_rows = orbitals.shape[1]
    positions = jnp.arange(NG, dtype=jnp.int32)
    places = np.arange(NG)
    high, low = (jnp.asarray(part) for part in split_table(cas_table(places[:, None], places[None, :])))

    def transform(axes, field):
        first = lax.reduce_precision(field, 8, 7)
        second = (field - first).astype(jnp.bfloat16)
        first = first.astype(jnp.bfloat16)
        return (
            jnp.einsum(axes, first, high, preferred_element_type=jnp.float32)
            + jnp.einsum(axes, first, low, preferred_element_type=jnp.float32)
            + jnp.einsum(axes, second, high, preferred_element_type=jnp.float32)
        )

    grid = orbitals.reshape(orbitals.shape[0], plane_rows, NG, NG)
    right = grid[pair_index[:, 1]].astype(jnp.float32)
    field = grid[pair_index[:, 0]].astype(jnp.float32) * right
    field = transform("pxyk,yv->pxvk", transform("pxyz,zk->pxyk", field))
    field = lax.all_to_all(field.astype(jnp.bfloat16), "pen", split_axis=2, concat_axis=1, tiled=True)
    col = signed_freq(lax.axis_index("pen") * slab + jnp.arange(slab, dtype=jnp.int32), NG)
    freq = signed_freq(positions, NG)
    square_sum = (freq * freq)[:, None, None] + (col * col)[None, :, None] + (freq * freq)[None, None, :]
    weights = coulomb_kernel(square_sum, NG) / float(NG * NG * NG)
    field = transform("pxyk,xv->pvyk", field.astype(jnp.float32)) * weights[None]
    field = transform("pxyk,xv->pvyk", field).astype(jnp.bfloat16)
    field = lax.all_to_all(field, "pen", split_axis=1, concat_axis=2, tiled=True)
    field = transform("pxyk,yv->pxvk", field.astype(jnp.float32))
    terms = transform("pxyk,kz->pxyz", field) * right
    return terms.reshape(terms.shape[0], plane_rows, NG * NG)


def tile_pass(tile_blocks, aux_local, pair_ids, live_count, contribute, initial):
    step_rows = 8

    def add_block(step_index, running):
        first_slot = step_index * step_rows
        tile_block = lax.dynamic_slice_in_dim(tile_blocks, first_slot, step_rows, 0)
        aux_block = lax.dynamic_slice_in_dim(aux_local, first_slot, step_rows, 0)
        pair_block = lax.dynamic_slice_in_dim(pair_ids, first_slot, step_rows, 0)
        slot_ids = first_slot + jnp.arange(step_rows, dtype=jnp.int32)
        live_mask = (slot_ids < live_count).astype(jnp.float32)
        return contribute(running, tile_block, aux_block, pair_block, live_mask)

    block_count = (live_count + step_rows - 1) // step_rows
    return lax.fori_loop(0, block_count, add_block, initial)


def coulomb_partial(tile_blocks, tile_aux, tile_pair, tile_count, density, metric_inv):
    aux_count = metric_inv.shape[0]
    dens_all = lax.all_gather(density, "blk", axis=0, tiled=True)
    aux_local = tile_aux - lax.axis_index("pen") * aux_count
    live_count = tile_count[0]
    aux_ids = jnp.arange(aux_count, dtype=jnp.int32)

    def add_fit(running, tile_block, aux_block, pair_block, live_mask):
        dens_rows = dens_all[pair_block]
        partial_value = jnp.einsum("tap,tp->ta", tile_block, dens_rows, preferred_element_type=jnp.float32)
        partial_value = partial_value * live_mask[:, None]
        selector = (aux_block[:, None] == aux_ids[None, :]).astype(jnp.float32)
        return running + jnp.einsum("tk,ta->ka", selector, partial_value, precision=PRECISE)

    gamma = jnp.zeros((aux_count, tile_blocks.shape[1]), jnp.float32)
    gamma = tile_pass(tile_blocks, aux_local, tile_pair, live_count, add_fit, gamma)
    gamma_all = lax.psum(gamma, ("grp", "blk"))
    coef = jnp.einsum("kab,kb->ka", metric_inv, gamma_all, precision=PRECISE).astype(jnp.bfloat16)

    def add_coulomb(running, tile_block, aux_block, pair_block, live_mask):
        selector = (aux_block[:, None] == aux_ids[None, :]).astype(jnp.bfloat16)
        coef_rows = jnp.dot(selector, coef, preferred_element_type=jnp.float32).astype(jnp.bfloat16)
        partial_value = jnp.einsum("tap,ta->tp", tile_block, coef_rows, preferred_element_type=jnp.float32)
        partial_value = partial_value * live_mask[:, None]
        return running.at[pair_block].add(partial_value)

    part = jnp.zeros((dens_all.shape[0], tile_blocks.shape[2]), jnp.float32)
    return tile_pass(tile_blocks, aux_local, tile_pair, live_count, add_coulomb, part)


def body(tile_blocks, tile_aux, tile_pair, tile_count, density, metric_inv, orbitals, pair_index):
    pen, blk, grp = (lax.axis_size(name) for name in ("pen", "blk", "grp"))
    slab = orbitals.shape[1]
    rows = density.shape[0] // (grp * pen)
    tiles = (tile_blocks, tile_aux, tile_pair, tile_count)
    if slab % ROWS == 0 and pen & (pen - 1) == 0 and pen >= NEAR and rows <= ROWS // 3:

        def coulomb_part(after):
            late_density, _ = lax.optimization_barrier((density, after))
            return coulomb_partial(*tiles, late_density, metric_inv), sum_part

        def sum_part(local):
            shares = local.reshape(grp, pen, blk, rows, LANE).transpose(0, 2, 1, 3, 4)
            shares = shares.reshape(grp * blk, pen * rows, LANE)
            taken = lax.all_to_all(shares, ("grp", "blk"), split_axis=0, concat_axis=0, tiled=True)
            return taken.sum(axis=0).reshape(pen, rows, LANE)

        return both_parts(orbitals, pair_index, pen, coulomb_part)
    part = coulomb_partial(*tiles, density, metric_inv)
    coulomb = lax.psum_scatter(part, ("grp", "pen", "blk"), scatter_dimension=0, tiled=True)
    return coulomb, pair_fields_plain(orbitals, pair_index, pen)


def solution(mesh):
    placed = (
        P(("grp", "pen", "blk"), None, None),
        P(("grp", "pen", "blk")),
        P(("grp", "pen", "blk")),
        P(("grp", "pen", "blk")),
        P("blk", None),
        P("pen", None, None),
        P(None, "pen", None),
        P(("grp", "blk"), None),
    )
    return jax.shard_map(
        body,
        mesh=mesh,
        in_specs=placed,
        out_specs=(P(("grp", "pen", "blk"), None), P(("grp", "blk"), "pen", None)),
        check_vma=False,
    )
```

```python
import functools
import math

import jax
import jax.numpy as jnp
import ml_dtypes
import numpy as np
from jax import lax
from jax.experimental import pallas as pl
from jax.experimental.pallas import tpu as pltpu
from jax.sharding import PartitionSpec as P

NG = 192
LANE = 128
TAIL = NG - LANE
PAIR_LANES = 2 * NG
ROWS = 16
NEAR = 2
UNROLL = 4

PRECISE = lax.Precision.HIGHEST
SPACING = 0.1348
VMEM_BYTES = 32 * 1024 * 1024
TILE_VMEM_BYTES = 16 * 1024 * 1024
VMEM_FIRST = 56 * 1024 * 1024


def signed_freq(position, length):
    return jnp.where(position < length // 2, position, position - length)


def coulomb_kernel(square_sum, length):
    box_length = SPACING * length
    kernel_scale = box_length * box_length / math.pi
    squares = square_sum.astype(jnp.float32)
    magnitude = jnp.sqrt(squares)
    denominator = jnp.where(square_sum == 0, 1.0, squares)
    regular = kernel_scale * (1.0 - jnp.cos(math.pi * magnitude)) / denominator
    return jnp.where(square_sum == 0, kernel_scale * math.pi * math.pi / 2.0, regular)


def cas_table(left, right):
    angles = (left * right % NG) * (2.0 * math.pi / NG)
    return np.cos(angles) + np.sin(angles)


def split_table(table):
    high = table.astype(ml_dtypes.bfloat16)
    return high, (table - high.astype(np.float64)).astype(ml_dtypes.bfloat16)


def split(values):
    high = values.astype(jnp.bfloat16)
    low = (values - high.astype(jnp.float32)).astype(jnp.bfloat16)
    return high, low


def split_rest(values):
    high = values.astype(jnp.bfloat16).astype(jnp.float32)
    return high, values - high


def width_of(slab):
    return slab * NG


def dot32(left, right):
    return jnp.dot(left, right, preferred_element_type=jnp.float32)


def split_dot(values, high_weight, low_weight):
    high, low = split(values)
    return dot32(high, high_weight) + dot32(high, low_weight) + dot32(low, high_weight)


def stacked_dot(stacked, values):
    count = stacked.shape[0] // 2
    high, low = split(values)
    both = dot32(stacked, high)
    return both[:count] + both[count:] + dot32(stacked[:count], low)


def stacked_dot_exact(stacked, values):
    count = stacked.shape[0] // 2
    both = dot32(stacked, values)
    return both[:count] + both[count:]


def forward_kernel(slab, pen, pairs_ref, left_ref, right_ref, depth_ref, cols_ref, *refs):
    outs, (rows_ref, head_ref, tail_ref, rest_ref) = refs[-4 - pen : -4], refs[-4:]
    half = NG // 2
    chunk = 32

    def depth_step(step, carry):
        start = pl.multiple_of(step * (chunk * PAIR_LANES), LANE)
        lanes = pl.ds(start, chunk * PAIR_LANES)
        field = left_ref[0, :, lanes].astype(jnp.float32) * right_ref[0, :, lanes].astype(jnp.float32)
        high, low = split(field)
        for parity in range(2):
            parts = []
            for source in (high, low):
                first = parity * LANE
                parts.append(
                    jnp.concatenate(
                        [source[:, k * PAIR_LANES + first : k * PAIR_LANES + first + 2 * LANE] for k in range(chunk)], axis=0
                    )
                )
            table_high, table_low = depth_ref[parity, 0], depth_ref[parity, 1]
            result = dot32(parts[0], table_high) + dot32(parts[0], table_low) + dot32(parts[1], table_high)
            place = pl.ds(pl.multiple_of((parity * half + step * chunk) * ROWS, ROWS), chunk * ROWS)
            rows_ref[0, place, :] = result[:, :LANE]
            rows_ref[1, place, :] = result[:, LANE:]
        return carry

    lax.fori_loop(0, half // chunk, depth_step, 0)
    low_lanes = lax.broadcasted_iota(jnp.int32, (slab // 2, LANE), 1) < TAIL

    @pl.when(pl.program_id(0) == 0)
    def _():
        rest_ref[...] = jnp.zeros_like(rest_ref)

    def rounded(values, place):
        values = values + rest_ref[place, :]
        kept = values.astype(jnp.bfloat16).astype(jnp.float32)
        rest_ref[place, :] = values - kept
        return kept

    def cols_step(plane, carry):
        strided = pl.ds(plane, NG, stride=ROWS)
        field = jnp.concatenate([rows_ref[0, strided, :], rows_ref[1, strided, :]], axis=1)
        result = stacked_dot(cols_ref[...], field)
        head_ref[strided, :] = rounded(result[:, :LANE], pl.ds(0, NG))
        tails = []
        for q in range(pen):
            first = result[q * slab : q * slab + slab // 2, LANE:]
            second = result[q * slab + slab // 2 : (q + 1) * slab, LANE:]
            tails.append(jnp.where(low_lanes, first, second))
        tail_ref[pl.ds(plane, half, stride=ROWS), :] = rounded(jnp.concatenate(tails, axis=0), pl.ds(NG, half))
        return carry

    lax.fori_loop(0, ROWS, cols_step, 0, unroll=UNROLL)
    for s in range(pen):
        owner = lax.axis_index("pen") ^ s
        for r in range(slab):
            place = pl.ds(pl.multiple_of((owner * slab + r) * ROWS, ROWS), ROWS)
            outs[s][:, r * LANE : (r + 1) * LANE] = head_ref[place, :].astype(jnp.bfloat16)
        for r in range(slab // 2):
            place = pl.ds(pl.multiple_of((owner * (slab // 2) + r) * ROWS, ROWS), ROWS)
            outs[s][:, (slab + r) * LANE : (slab + r + 1) * LANE] = tail_ref[place, :].astype(jnp.bfloat16)


def middle_kernel(pen, in_pieces, out_pieces, extra, in_ref, out_table_ref, grid_ref, part_ref, *refs):
    fields, outs, planes_ref = refs[: len(in_pieces)], refs[len(in_pieces) : -1], refs[-1]
    slab = NG // pen
    block = planes_ref.shape[1]

    def place(s, first, count):
        return pl.ds(pl.multiple_of((lax.axis_index("pen") ^ s) * slab + first, ROWS), count)

    for field, piece in zip(fields, in_pieces):
        planes_ref[place(*piece), :] = field[...]
    half = NG // 2
    weights = grid_ref[:half, :]
    top = lax.broadcasted_iota(jnp.int32, (ROWS // 2, block), 0) == 0
    mirrored = jnp.where(top, grid_ref[half:, :], weights[: ROWS // 2])
    weights = jnp.concatenate([weights, mirrored, weights[ROWS // 2 :]], axis=0)
    spectral = stacked_dot_exact(in_ref[...], planes_ref[...]) * weights
    planes_ref[...] = stacked_dot(out_table_ref[...], spectral).astype(jnp.bfloat16)
    for out_ref, piece in zip(outs, out_pieces):
        values = planes_ref[place(*piece), :]
        if not (extra and piece[1] + piece[2] == slab):
            out_ref[...] = values
            continue
        lanes = pl.ds(pl.multiple_of(pl.program_id(0) * block, LANE), block)
        out_ref[:, lanes] = values
        high, rest = split_rest(part_ref[lax.axis_index("pen") ^ piece[0]])
        middle, rest = split_rest(rest)
        blank = jnp.zeros((ROWS - 3 * high.shape[0], LANE), jnp.float32)
        if piece[2] > ROWS:
            out_ref[: piece[2] - ROWS, width_of(slab) :] = jnp.zeros((piece[2] - ROWS, LANE), jnp.bfloat16)
        tag = jnp.concatenate([high, middle, rest, blank], axis=0).astype(jnp.bfloat16)
        out_ref[piece[2] - ROWS :, width_of(slab) :] = tag


def inverse_kernel(slab, pen, extra, pairs_ref, *refs):
    fields = refs[:pen]
    right_ref, cols_ref, depth_ref = refs[pen : pen + 3]
    out_ref, rows_ref, head_ref, tail_ref = refs[-4:]
    if extra:
        part_ref, out_ref = refs[-4], refs[-5]
        rows = part_ref.shape[0]
        tags = [field[:, width_of(slab) :].astype(jnp.float32) for field in fields]
        part_ref[...] = sum(tag[c * rows : (c + 1) * rows] for c in (2, 1, 0) for tag in tags)
    half = NG // 2
    chunk = 32
    for s in range(pen):
        owner = lax.axis_index("pen") ^ s
        for r in range(slab):
            place = pl.ds(pl.multiple_of((owner * slab + r) * ROWS, ROWS), ROWS)
            head_ref[place, :] = fields[s][:, r * LANE : (r + 1) * LANE].astype(jnp.float32)
        for r in range(slab // 2):
            place = pl.ds(pl.multiple_of((owner * (slab // 2) + r) * ROWS, ROWS), ROWS)
            tail_ref[place, :] = fields[s][:, (slab + r) * LANE : (slab + r + 1) * LANE].astype(jnp.float32)
    low_lanes = lax.broadcasted_iota(jnp.int32, (slab // 2, LANE), 1) < TAIL

    def cols_step(plane, carry):
        strided = pl.ds(plane, NG, stride=ROWS)
        tail = tail_ref[pl.ds(plane, half, stride=ROWS), :]
        pieces = []
        for q in range(pen):
            both = tail[q * (slab // 2) : (q + 1) * (slab // 2)]
            pieces.append(jnp.where(low_lanes, both, 0.0))
            pieces.append(jnp.where(low_lanes, 0.0, both))
        field = jnp.concatenate([head_ref[strided, :], jnp.concatenate(pieces, axis=0)], axis=1)
        result = stacked_dot_exact(cols_ref[...], field.astype(jnp.bfloat16))
        rows_ref[0, strided, :] = result[:, :LANE]
        rows_ref[1, strided, :] = result[:, LANE:]
        return carry

    lax.fori_loop(0, ROWS, cols_step, 0, unroll=UNROLL)

    def depth_step(step, carry):
        results = []
        for parity in range(2):
            place = pl.ds(pl.multiple_of((parity * half + step * chunk) * ROWS, ROWS), chunk * ROWS)
            field = jnp.concatenate([rows_ref[0, place, :], rows_ref[1, place, :]], axis=1)
            results.append(split_dot(field, depth_ref[parity, 0], depth_ref[parity, 1]))
        for k in range(chunk):
            even, odd = (value[k * ROWS : (k + 1) * ROWS] for value in results)
            potential = jnp.concatenate([even[:, :LANE], even[:, LANE:] + odd[:, :LANE], odd[:, LANE:]], axis=1)
            lanes = pl.ds(pl.multiple_of((step * chunk + k) * PAIR_LANES, LANE), PAIR_LANES)
            out_ref[0, :, lanes] = potential * right_ref[0, :, lanes].astype(jnp.float32)
        return carry

    lax.fori_loop(0, half // chunk, depth_step, 0)


def fit_kernel(aux_ref, slots_ref, count_ref, tiles_ref, density_ref, gamma_ref, rows_ref):
    rows_ref[...] = density_ref[...].astype(jnp.float32)
    gamma_ref[...] = jnp.zeros_like(gamma_ref)
    base = lax.axis_index("pen") * gamma_ref.shape[0]
    for t in range(tiles_ref.shape[0]):
        row = jnp.broadcast_to(rows_ref[pl.ds(slots_ref[t], 1), :], (ROWS, LANE)).astype(jnp.bfloat16)
        value = lax.dot_general(row, tiles_ref[t], (((1,), (1,)), ((), ())), preferred_element_type=jnp.float32)
        place = pl.ds(aux_ref[t] - base, 1)
        gamma_ref[place, :] += jnp.where(t < count_ref[0], value[:1], 0.0)


def build_kernel(aux_ref, slots_ref, count_ref, tiles_ref, coef_ref, part_ref):
    part_ref[...] = jnp.zeros_like(part_ref)
    base = lax.axis_index("pen") * coef_ref.shape[0]
    for t in range(tiles_ref.shape[0]):
        row = jnp.broadcast_to(coef_ref[pl.ds(aux_ref[t] - base, 1), :], (ROWS, LANE)).astype(jnp.bfloat16)
        value = dot32(row, tiles_ref[t])
        place = pl.ds(slots_ref[t], 1)
        part_ref[place, :] += jnp.where(t < count_ref[0], value[:1], 0.0)


def tile_call(kernel, tiles, rows, out_rows, scratch, name):
    tile_blocks, tile_aux, tile_pair, tile_count = tiles
    return pl.pallas_call(
        kernel,
        out_shape=jax.ShapeDtypeStruct((out_rows, LANE), jnp.float32),
        grid_spec=pltpu.PrefetchScalarGridSpec(
            num_scalar_prefetch=3,
            grid=(1,),
            in_specs=[whole_spec(tile_blocks.shape), whole_spec(rows.shape)],
            out_specs=whole_spec((out_rows, LANE)),
            scratch_shapes=scratch,
        ),
        compiler_params=pltpu.CompilerParams(vmem_limit_bytes=TILE_VMEM_BYTES),
        cost_estimate=pl.CostEstimate(
            flops=2 * tile_blocks.size * ROWS, bytes_accessed=2 * tile_blocks.size, transcendentals=0
        ),
        name=name,
    )(tile_aux, tile_pair, tile_count, tile_blocks, rows)


def whole_spec(shape):
    return pl.BlockSpec(shape, lambda *_: (0,) * len(shape))


def column_scratch():
    return [
        pltpu.VMEM((2, NG * ROWS, LANE), jnp.float32),
        pltpu.VMEM((NG * ROWS, LANE), jnp.float32),
        pltpu.VMEM((NG // 2 * ROWS, LANE), jnp.float32),
    ]


def forward_planes(pair_index, pair, orbitals, depth_tables, cols_table, pen, first, count, earlier, after):
    slab = NG // pen
    width = width_of(slab)
    skip = first // ROWS
    near = jax.ShapeDtypeStruct((slab, width), jnp.bfloat16)
    far = jax.ShapeDtypeStruct((count, width), jnp.bfloat16)
    operands = [pair_index, orbitals, orbitals, depth_tables, cols_table]
    aliases = {len(operands) + s: s for s in range(len(earlier))}
    operands += [*earlier, *after]
    return pl.pallas_call(
        functools.partial(forward_kernel, slab, pen),
        out_shape=[near] * NEAR + [far] * (pen - NEAR),
        grid_spec=pltpu.PrefetchScalarGridSpec(
            num_scalar_prefetch=1,
            grid=(count // ROWS,),
            in_specs=[
                pl.BlockSpec((1, ROWS, NG * NG), lambda b, pairs: (pairs[pair, 0], b + skip, 0)),
                pl.BlockSpec((1, ROWS, NG * NG), lambda b, pairs: (pairs[pair, 1], b + skip, 0)),
                whole_spec(depth_tables.shape),
                whole_spec(cols_table.shape),
            ]
            + [pl.BlockSpec(memory_space=pl.ANY)] * (len(earlier) + len(after)),
            out_specs=[pl.BlockSpec((ROWS, width), lambda b, *_: (b + skip, 0))] * NEAR
            + [pl.BlockSpec((ROWS, width), lambda b, *_: (b, 0))] * (pen - NEAR),
            scratch_shapes=column_scratch() + [pltpu.VMEM((NG + NG // 2, LANE), jnp.float32)],
        ),
        input_output_aliases=aliases,
        compiler_params=pltpu.CompilerParams(vmem_limit_bytes=VMEM_BYTES if earlier else VMEM_FIRST),
        cost_estimate=pl.CostEstimate(
            flops=2 * 6 * count * NG * NG * NG, bytes_accessed=6 * count * NG * NG, transcendentals=0
        ),
        name="forward_planes",
    )(*operands)


def middle_columns(fields, in_pieces, tables, grid_table, part, pen, out_pieces, extra):
    slab = NG // pen
    width = width_of(slab)
    block = width // 8
    out_shapes, out_specs = [], []
    for s, first, count in out_pieces:
        if extra and first + count == slab:
            out_shapes.append(jax.ShapeDtypeStruct((count, width + LANE), jnp.bfloat16))
            out_specs.append(whole_spec((count, width + LANE)))
        else:
            out_shapes.append(jax.ShapeDtypeStruct((count, width), jnp.bfloat16))
            out_specs.append(pl.BlockSpec((count, block), lambda b, *_: (0, b)))
    in_specs = [whole_spec(table.shape) for table in tables]
    in_specs += [pl.BlockSpec((grid_table.shape[0], block), lambda b, *_: (0, b)), whole_spec(part.shape)]
    in_specs += [pl.BlockSpec((count, block), lambda b, *_: (0, b)) for s, first, count in in_pieces]
    return pl.pallas_call(
        functools.partial(middle_kernel, pen, in_pieces, out_pieces, extra),
        out_shape=out_shapes,
        grid=(width // block,),
        in_specs=in_specs,
        out_specs=out_specs,
        scratch_shapes=[pltpu.VMEM((NG, block), jnp.bfloat16)],
        compiler_params=pltpu.CompilerParams(vmem_limit_bytes=VMEM_BYTES),
        cost_estimate=pl.CostEstimate(flops=2 * 5 * NG * NG * width, bytes_accessed=8 * NG * width, transcendentals=0),
        name="middle_columns",
    )(*tables, grid_table, part, *fields)


def inverse_planes(pair_index, pair, fields, orbitals, cols_table, depth_tables, first, earlier, part_rows):
    pen = len(fields)
    slab = NG // pen
    count = fields[-1].shape[0]
    skip = first // ROWS
    out_shapes = [jax.ShapeDtypeStruct((pair_index.shape[0], slab, NG * NG), jnp.float32)]
    out_specs = [pl.BlockSpec((1, ROWS, NG * NG), lambda b, *_: (pair, b + skip, 0))]
    if part_rows:
        out_shapes.append(jax.ShapeDtypeStruct((part_rows, LANE), jnp.float32))
        out_specs.append(whole_spec((part_rows, LANE)))
    in_specs = [pl.BlockSpec((ROWS, field.shape[1]), lambda b, *_: (b + skip, 0)) for field in fields[:NEAR]]
    in_specs += [pl.BlockSpec((ROWS, field.shape[1]), lambda b, *_: (b, 0)) for field in fields[NEAR:]]
    in_specs += [
        pl.BlockSpec((1, ROWS, NG * NG), lambda b, pairs: (pairs[pair, 1], b + skip, 0)),
        whole_spec(cols_table.shape),
        whole_spec(depth_tables.shape),
    ]
    operands = [pair_index, *fields, orbitals, cols_table, depth_tables]
    aliases = {}
    if earlier is not None:
        aliases = {len(operands): 0}
        in_specs.append(pl.BlockSpec(memory_space=pl.ANY))
        operands.append(earlier)
    return pl.pallas_call(
        functools.partial(inverse_kernel, slab, pen, bool(part_rows)),
        out_shape=out_shapes,
        grid_spec=pltpu.PrefetchScalarGridSpec(
            num_scalar_prefetch=1,
            grid=(count // ROWS,),
            in_specs=in_specs,
            out_specs=out_specs,
            scratch_shapes=column_scratch(),
        ),
        input_output_aliases=aliases,
        compiler_params=pltpu.CompilerParams(vmem_limit_bytes=VMEM_BYTES),
        cost_estimate=pl.CostEstimate(
            flops=2 * 5 * count * NG * NG * NG, bytes_accessed=8 * count * NG * NG, transcendentals=0
        ),
        name="inverse_planes",
    )(*operands)


def exchange(s, field, pen):
    return lax.ppermute(field, "pen", [(i, i ^ s) for i in range(pen)]) if s else field


def stack_split(table):
    return np.concatenate(split_table(table), axis=0)


def depth_table_set():
    lanes = np.arange(2 * LANE)
    freq = np.where(lanes < NG, lanes, lanes - TAIL)
    tables = []
    for parity in range(2):
        depth = lanes - parity * TAIL
        inside = (depth >= 0) & (depth < NG)
        tables.append(np.where(inside[:, None], cas_table(depth[:, None], freq[None, :]), 0.0))
    return np.stack(split_table(np.stack(tables)), axis=1)


def grid_weights(me, slab):
    lane = jnp.arange(LANE, dtype=jnp.int32)[None, :]
    row = jnp.arange(slab, dtype=jnp.int32)[:, None]
    head_col, head_depth = jnp.broadcast_arrays(row, lane)
    tail_row = row[: slab // 2]
    tail_col = jnp.where(lane < TAIL, tail_row, tail_row + slab // 2)
    tail_depth = jnp.broadcast_to(LANE + lane % TAIL, tail_col.shape)
    col = signed_freq(me * slab + jnp.concatenate([head_col, tail_col], axis=0).reshape(-1), NG)
    depth = signed_freq(jnp.concatenate([head_depth, tail_depth], axis=0).reshape(-1), NG)
    plane = jnp.arange(NG // 2 + ROWS // 2, dtype=jnp.int32)
    square_sum = (plane * plane)[:, None] + (col * col + depth * depth)[None, :]
    return coulomb_kernel(square_sum, NG) / float(NG * NG * NG)


def plane_frequencies():
    upper = (NG - np.arange(NG // 2)) % NG
    upper[0] = NG // 2
    return np.concatenate([np.arange(NG // 2), upper])


def plane_runs(slab, first, last):
    if slab > ROWS and first:
        return ((0, ROWS), (ROWS, slab - ROWS))
    if slab > ROWS and last:
        return ((0, slab - ROWS), (slab - ROWS, ROWS))
    return ((0, slab),)


def pieces_of(pen, runs):
    far = tuple((s, first, count) for first, count in runs for s in range(pen - 1, NEAR - 1, -1))
    return far + tuple((s, 0, NG // pen) for s in range(NEAR - 1, -1, -1))


def both_parts(orbitals, pair_index, pen, coulomb_local, coulomb_part):
    slab = NG // pen
    pairs = pair_index.shape[0]
    me = lax.axis_index("pen").astype(jnp.int32)
    positions = np.arange(NG)
    interleaved = np.concatenate([positions[0::2], positions[1::2]])
    depth_np = depth_table_set()
    depth_tables, depth_back = jnp.asarray(depth_np), jnp.asarray(np.swapaxes(depth_np, 2, 3))
    cols_forward = jnp.asarray(stack_split(cas_table(positions[:, None], interleaved[None, :])))
    cols_back = jnp.asarray(stack_split(cas_table(interleaved[:, None], positions[None, :])))
    frequencies = plane_frequencies()
    plane_tables = (
        jnp.asarray(stack_split(cas_table(frequencies[:, None], positions[None, :]))),
        jnp.asarray(stack_split(cas_table(positions[:, None], frequencies[None, :]))),
    )

    held, after = [], []
    for p in range(pairs):
        runs = plane_runs(slab, p == 0, False)
        taken, made = {}, ()
        for first, count in runs:
            made = forward_planes(
                pair_index, p, orbitals, depth_tables, cols_forward, pen, first, count, made[:NEAR], after if first == 0 else ()
            )
            for s in range(NEAR, pen):
                taken[s, first] = exchange(s, made[s], pen)
            if p == 0 and first == 0:
                local = coulomb_local(made[-1])
        for s in range(NEAR):
            taken[s, 0] = exchange(s, made[s], pen)
        pieces = pieces_of(pen, runs)
        held.append((pieces, [taken[s, first] for s, first, count in pieces]))
        if p == 0:
            late_me, _ = lax.optimization_barrier((me, made[-1]))
            grid_table = grid_weights(late_me, slab)
            after = [grid_table, local]
    part = coulomb_part(local)

    back = []
    for p in range(pairs):
        last = p == pairs - 1
        fed = part if last else jnp.zeros_like(part)
        runs = plane_runs(slab, False, last)
        pieces = pieces_of(pen, runs)
        filtered = middle_columns(held[p][1], held[p][0], plane_tables, grid_table, fed, pen, pieces, last)
        back.append((runs, {piece[:2]: exchange(piece[0], field, pen) for piece, field in zip(pieces, filtered)}))

    terms = None
    for p in range(pairs):
        runs, taken = back[p]
        for first, count in runs:
            final = p == pairs - 1 and first + count == slab
            fields = [taken[s, 0 if s < NEAR else first] for s in range(pen)]
            made = inverse_planes(
                pair_index, p, fields, orbitals, cols_back, depth_back, first, terms, part.shape[1] if final else 0
            )
            terms = made[0]
    return made[1], terms


def pair_fields_plain(orbitals, pair_index, pen):
    slab = NG // pen
    plane_rows = orbitals.shape[1]
    positions = jnp.arange(NG, dtype=jnp.int32)
    places = np.arange(NG)
    high, low = (jnp.asarray(part) for part in split_table(cas_table(places[:, None], places[None, :])))

    def transform(axes, field):
        first = lax.reduce_precision(field, 8, 7)
        second = (field - first).astype(jnp.bfloat16)
        first = first.astype(jnp.bfloat16)
        return (
            jnp.einsum(axes, first, high, preferred_element_type=jnp.float32)
            + jnp.einsum(axes, first, low, preferred_element_type=jnp.float32)
            + jnp.einsum(axes, second, high, preferred_element_type=jnp.float32)
        )

    grid = orbitals.reshape(orbitals.shape[0], plane_rows, NG, NG)
    right = grid[pair_index[:, 1]].astype(jnp.float32)
    field = grid[pair_index[:, 0]].astype(jnp.float32) * right
    field = transform("pxyk,yv->pxvk", transform("pxyz,zk->pxyk", field))
    field = lax.all_to_all(field.astype(jnp.bfloat16), "pen", split_axis=2, concat_axis=1, tiled=True)
    col = signed_freq(lax.axis_index("pen") * slab + jnp.arange(slab, dtype=jnp.int32), NG)
    freq = signed_freq(positions, NG)
    square_sum = (freq * freq)[:, None, None] + (col * col)[None, :, None] + (freq * freq)[None, None, :]
    weights = coulomb_kernel(square_sum, NG) / float(NG * NG * NG)
    field = transform("pxyk,xv->pvyk", field.astype(jnp.float32)) * weights[None]
    field = transform("pxyk,xv->pvyk", field).astype(jnp.bfloat16)
    field = lax.all_to_all(field, "pen", split_axis=1, concat_axis=2, tiled=True)
    field = transform("pxyk,yv->pxvk", field.astype(jnp.float32))
    terms = transform("pxyk,kz->pxyz", field) * right
    return terms.reshape(terms.shape[0], plane_rows, NG * NG)


def tile_pass(tile_blocks, aux_local, pair_ids, live_count, contribute, initial):
    step_rows = 8

    def add_block(step_index, running):
        first_slot = step_index * step_rows
        tile_block = lax.dynamic_slice_in_dim(tile_blocks, first_slot, step_rows, 0)
        aux_block = lax.dynamic_slice_in_dim(aux_local, first_slot, step_rows, 0)
        pair_block = lax.dynamic_slice_in_dim(pair_ids, first_slot, step_rows, 0)
        slot_ids = first_slot + jnp.arange(step_rows, dtype=jnp.int32)
        live_mask = (slot_ids < live_count).astype(jnp.float32)
        return contribute(running, tile_block, aux_block, pair_block, live_mask)

    block_count = (live_count + step_rows - 1) // step_rows
    return lax.fori_loop(0, block_count, add_block, initial)


def to_all(values, count, axes):
    copies = jnp.broadcast_to(values[None], (count, *values.shape))
    return lax.all_to_all(copies, axes, split_axis=0, concat_axis=0, tiled=True)


def coulomb_partial(tile_blocks, tile_aux, tile_pair, tile_count, density, metric_inv):
    aux_count = metric_inv.shape[0]
    dens_all = lax.all_gather(density, "blk", axis=0, tiled=True)
    aux_local = tile_aux - lax.axis_index("pen") * aux_count
    live_count = tile_count[0]
    aux_ids = jnp.arange(aux_count, dtype=jnp.int32)

    def add_fit(running, tile_block, aux_block, pair_block, live_mask):
        dens_rows = dens_all[pair_block]
        partial_value = jnp.einsum("tap,tp->ta", tile_block, dens_rows, preferred_element_type=jnp.float32)
        partial_value = partial_value * live_mask[:, None]
        selector = (aux_block[:, None] == aux_ids[None, :]).astype(jnp.float32)
        return running + jnp.einsum("tk,ta->ka", selector, partial_value, precision=PRECISE)

    gamma = jnp.zeros((aux_count, tile_blocks.shape[1]), jnp.float32)
    gamma = tile_pass(tile_blocks, aux_local, tile_pair, live_count, add_fit, gamma)
    gamma_all = lax.psum(gamma, ("grp", "blk"))
    coef = jnp.einsum("kab,kb->ka", metric_inv, gamma_all, precision=PRECISE).astype(jnp.bfloat16)

    def add_coulomb(running, tile_block, aux_block, pair_block, live_mask):
        selector = (aux_block[:, None] == aux_ids[None, :]).astype(jnp.bfloat16)
        coef_rows = jnp.dot(selector, coef, preferred_element_type=jnp.float32).astype(jnp.bfloat16)
        partial_value = jnp.einsum("tap,ta->tp", tile_block, coef_rows, preferred_element_type=jnp.float32)
        partial_value = partial_value * live_mask[:, None]
        return running.at[pair_block].add(partial_value)

    part = jnp.zeros((dens_all.shape[0], tile_blocks.shape[2]), jnp.float32)
    return tile_pass(tile_blocks, aux_local, tile_pair, live_count, add_coulomb, part)


def body(tile_blocks, tile_aux, tile_pair, tile_count, density, metric_inv, orbitals, pair_index):
    pen, blk, grp = (lax.axis_size(name) for name in ("pen", "blk", "grp"))
    slab = orbitals.shape[1]
    rows = density.shape[0] // (grp * pen)
    tiles = (tile_blocks, tile_aux, tile_pair, tile_count)
    if slab % ROWS == 0 and pen & (pen - 1) == 0 and pen >= NEAR and rows <= ROWS // 3:

        def coulomb_local(after):
            late_density, _ = lax.optimization_barrier((density, after))
            dens_all = to_all(late_density, blk, "blk").reshape(-1, LANE)
            scratch = [pltpu.VMEM(dens_all.shape, jnp.float32)]
            gamma = tile_call(fit_kernel, tiles, dens_all, metric_inv.shape[0], scratch, "fit_tiles")
            gamma = to_all(gamma, grp * blk, ("grp", "blk")).sum(axis=0)
            coef = jnp.einsum("kab,kb->ka", metric_inv, gamma, precision=PRECISE)
            coef = lax.reduce_precision(coef, 8, 7)
            return tile_call(build_kernel, tiles, coef, dens_all.shape[0], [], "build_tiles")

        def coulomb_part(local):
            shares = local.reshape(grp, pen, blk, rows, LANE).transpose(0, 2, 1, 3, 4)
            shares = shares.reshape(grp * blk, pen * rows, LANE)
            taken = lax.all_to_all(shares, ("grp", "blk"), split_axis=0, concat_axis=0, tiled=True)
            return taken.sum(axis=0).reshape(pen, rows, LANE)

        return both_parts(orbitals, pair_index, pen, coulomb_local, coulomb_part)
    part = coulomb_partial(*tiles, density, metric_inv)
    coulomb = lax.psum_scatter(part, ("grp", "pen", "blk"), scatter_dimension=0, tiled=True)
    return coulomb, pair_fields_plain(orbitals, pair_index, pen)


def solution(mesh):
    placed = (
        P(("grp", "pen", "blk"), None, None),
        P(("grp", "pen", "blk")),
        P(("grp", "pen", "blk")),
        P(("grp", "pen", "blk")),
        P("blk", None),
        P("pen", None, None),
        P(None, "pen", None),
        P(("grp", "blk"), None),
    )
    return jax.shard_map(
        body,
        mesh=mesh,
        in_specs=placed,
        out_specs=(P(("grp", "pen", "blk"), None), P(("grp", "blk"), "pen", None)),
        check_vma=False,
    )
```

```python
import functools
import math

import jax
import jax.numpy as jnp
import ml_dtypes
import numpy as np
from jax import lax
from jax.experimental import pallas as pl
from jax.experimental.pallas import tpu as pltpu
from jax.sharding import PartitionSpec as P

NG = 192
LANE = 128
TAIL = NG - LANE
PAIR_LANES = 2 * NG
ROWS = 16
NEAR = 2
UNROLL = 8

PRECISE = lax.Precision.HIGHEST
SPACING = 0.1348
VMEM_BYTES = 32 * 1024 * 1024
TILE_VMEM_BYTES = 16 * 1024 * 1024
VMEM_FIRST = 56 * 1024 * 1024


def signed_freq(position, length):
    return jnp.where(position < length // 2, position, position - length)


def coulomb_kernel(square_sum, length):
    box_length = SPACING * length
    kernel_scale = box_length * box_length / math.pi
    squares = square_sum.astype(jnp.float32)
    magnitude = jnp.sqrt(squares)
    denominator = jnp.where(square_sum == 0, 1.0, squares)
    regular = kernel_scale * (1.0 - jnp.cos(math.pi * magnitude)) / denominator
    return jnp.where(square_sum == 0, kernel_scale * math.pi * math.pi / 2.0, regular)


def cas_table(left, right):
    angles = (left * right % NG) * (2.0 * math.pi / NG)
    return np.cos(angles) + np.sin(angles)


def split_table(table):
    high = table.astype(ml_dtypes.bfloat16)
    return high, (table - high.astype(np.float64)).astype(ml_dtypes.bfloat16)


def split(values):
    high = values.astype(jnp.bfloat16)
    low = (values - high.astype(jnp.float32)).astype(jnp.bfloat16)
    return high, low


def split_rest(values):
    high = values.astype(jnp.bfloat16).astype(jnp.float32)
    return high, values - high


def width_of(slab):
    return slab * NG


def dot32(left, right):
    return jnp.dot(left, right, preferred_element_type=jnp.float32)


def split_dot(values, high_weight, low_weight):
    high, low = split(values)
    return dot32(high, high_weight) + dot32(high, low_weight) + dot32(low, high_weight)


def stacked_dot(stacked, values):
    count = stacked.shape[0] // 2
    high, low = split(values)
    both = dot32(stacked, high)
    return both[:count] + both[count:] + dot32(stacked[:count], low)


def stacked_dot_exact(stacked, values):
    count = stacked.shape[0] // 2
    both = dot32(stacked, values)
    return both[:count] + both[count:]


def forward_kernel(slab, pen, pairs_ref, left_ref, right_ref, depth_ref, cols_ref, *refs):
    outs, (rows_ref, head_ref, tail_ref, rest_ref) = refs[-4 - pen : -4], refs[-4:]
    half = NG // 2
    chunk = 32

    def depth_step(step, carry):
        start = pl.multiple_of(step * (chunk * PAIR_LANES), LANE)
        lanes = pl.ds(start, chunk * PAIR_LANES)
        field = left_ref[0, :, lanes].astype(jnp.float32) * right_ref[0, :, lanes].astype(jnp.float32)
        high, low = split(field)
        for parity in range(2):
            parts = []
            for source in (high, low):
                first = parity * LANE
                parts.append(
                    jnp.concatenate(
                        [source[:, k * PAIR_LANES + first : k * PAIR_LANES + first + 2 * LANE] for k in range(chunk)], axis=0
                    )
                )
            table_high, table_low = depth_ref[parity, 0], depth_ref[parity, 1]
            result = dot32(parts[0], table_high) + dot32(parts[0], table_low) + dot32(parts[1], table_high)
            place = pl.ds(pl.multiple_of((parity * half + step * chunk) * ROWS, ROWS), chunk * ROWS)
            rows_ref[0, place, :] = result[:, :LANE]
            rows_ref[1, place, :] = result[:, LANE:]
        return carry

    lax.fori_loop(0, half // chunk, depth_step, 0)
    low_lanes = lax.broadcasted_iota(jnp.int32, (slab // 2, LANE), 1) < TAIL

    @pl.when(pl.program_id(0) == 0)
    def _():
        rest_ref[...] = jnp.zeros_like(rest_ref)

    def rounded(values, place):
        values = values + rest_ref[place, :]
        kept = values.astype(jnp.bfloat16).astype(jnp.float32)
        rest_ref[place, :] = values - kept
        return kept

    def cols_step(plane, carry):
        strided = pl.ds(plane, NG, stride=ROWS)
        field = jnp.concatenate([rows_ref[0, strided, :], rows_ref[1, strided, :]], axis=1)
        result = stacked_dot(cols_ref[...], field)
        head_ref[strided, :] = rounded(result[:, :LANE], pl.ds(0, NG))
        tails = []
        for q in range(pen):
            first = result[q * slab : q * slab + slab // 2, LANE:]
            second = result[q * slab + slab // 2 : (q + 1) * slab, LANE:]
            tails.append(jnp.where(low_lanes, first, second))
        tail_ref[pl.ds(plane, half, stride=ROWS), :] = rounded(jnp.concatenate(tails, axis=0), pl.ds(NG, half))
        return carry

    lax.fori_loop(0, ROWS, cols_step, 0, unroll=UNROLL)
    for s in range(pen):
        owner = lax.axis_index("pen") ^ s
        for r in range(slab):
            place = pl.ds(pl.multiple_of((owner * slab + r) * ROWS, ROWS), ROWS)
            outs[s][:, r * LANE : (r + 1) * LANE] = head_ref[place, :].astype(jnp.bfloat16)
        for r in range(slab // 2):
            place = pl.ds(pl.multiple_of((owner * (slab // 2) + r) * ROWS, ROWS), ROWS)
            outs[s][:, (slab + r) * LANE : (slab + r + 1) * LANE] = tail_ref[place, :].astype(jnp.bfloat16)


def middle_kernel(pen, in_pieces, out_pieces, extra, in_ref, out_table_ref, grid_ref, part_ref, *refs):
    fields, outs, planes_ref = refs[: len(in_pieces)], refs[len(in_pieces) : -1], refs[-1]
    slab = NG // pen
    block = planes_ref.shape[1]

    def place(s, first, count):
        return pl.ds(pl.multiple_of((lax.axis_index("pen") ^ s) * slab + first, ROWS), count)

    for field, piece in zip(fields, in_pieces):
        planes_ref[place(*piece), :] = field[...]
    half = NG // 2
    weights = grid_ref[:half, :]
    top = lax.broadcasted_iota(jnp.int32, (ROWS // 2, block), 0) == 0
    mirrored = jnp.where(top, grid_ref[half:, :], weights[: ROWS // 2])
    weights = jnp.concatenate([weights, mirrored, weights[ROWS // 2 :]], axis=0)
    spectral = stacked_dot_exact(in_ref[...], planes_ref[...]) * weights
    planes_ref[...] = stacked_dot(out_table_ref[...], spectral).astype(jnp.bfloat16)
    for out_ref, piece in zip(outs, out_pieces):
        values = planes_ref[place(*piece), :]
        if not (extra and piece[1] + piece[2] == slab):
            out_ref[...] = values
            continue
        lanes = pl.ds(pl.multiple_of(pl.program_id(0) * block, LANE), block)
        out_ref[:, lanes] = values
        high, rest = split_rest(part_ref[lax.axis_index("pen") ^ piece[0]])
        middle, rest = split_rest(rest)
        blank = jnp.zeros((ROWS - 3 * high.shape[0], LANE), jnp.float32)
        if piece[2] > ROWS:
            out_ref[: piece[2] - ROWS, width_of(slab) :] = jnp.zeros((piece[2] - ROWS, LANE), jnp.bfloat16)
        tag = jnp.concatenate([high, middle, rest, blank], axis=0).astype(jnp.bfloat16)
        out_ref[piece[2] - ROWS :, width_of(slab) :] = tag


def inverse_kernel(slab, pen, extra, pairs_ref, *refs):
    fields = refs[:pen]
    right_ref, cols_ref, depth_ref = refs[pen : pen + 3]
    out_ref, rows_ref, head_ref, tail_ref = refs[-4:]
    if extra:
        part_ref, out_ref = refs[-4], refs[-5]
        rows = part_ref.shape[0]
        tags = [field[:, width_of(slab) :].astype(jnp.float32) for field in fields]
        part_ref[...] = sum(tag[c * rows : (c + 1) * rows] for c in (2, 1, 0) for tag in tags)
    half = NG // 2
    chunk = 32
    for s in range(pen):
        owner = lax.axis_index("pen") ^ s
        for r in range(slab):
            place = pl.ds(pl.multiple_of((owner * slab + r) * ROWS, ROWS), ROWS)
            head_ref[place, :] = fields[s][:, r * LANE : (r + 1) * LANE].astype(jnp.float32)
        for r in range(slab // 2):
            place = pl.ds(pl.multiple_of((owner * (slab // 2) + r) * ROWS, ROWS), ROWS)
            tail_ref[place, :] = fields[s][:, (slab + r) * LANE : (slab + r + 1) * LANE].astype(jnp.float32)
    low_lanes = lax.broadcasted_iota(jnp.int32, (slab // 2, LANE), 1) < TAIL

    def cols_step(plane, carry):
        strided = pl.ds(plane, NG, stride=ROWS)
        tail = tail_ref[pl.ds(plane, half, stride=ROWS), :]
        pieces = []
        for q in range(pen):
            both = tail[q * (slab // 2) : (q + 1) * (slab // 2)]
            pieces.append(jnp.where(low_lanes, both, 0.0))
            pieces.append(jnp.where(low_lanes, 0.0, both))
        field = jnp.concatenate([head_ref[strided, :], jnp.concatenate(pieces, axis=0)], axis=1)
        result = stacked_dot_exact(cols_ref[...], field.astype(jnp.bfloat16))
        rows_ref[0, strided, :] = result[:, :LANE]
        rows_ref[1, strided, :] = result[:, LANE:]
        return carry

    lax.fori_loop(0, ROWS, cols_step, 0, unroll=UNROLL)

    def depth_step(step, carry):
        results = []
        for parity in range(2):
            place = pl.ds(pl.multiple_of((parity * half + step * chunk) * ROWS, ROWS), chunk * ROWS)
            field = jnp.concatenate([rows_ref[0, place, :], rows_ref[1, place, :]], axis=1)
            results.append(split_dot(field, depth_ref[parity, 0], depth_ref[parity, 1]))
        for k in range(chunk):
            even, odd = (value[k * ROWS : (k + 1) * ROWS] for value in results)
            potential = jnp.concatenate([even[:, :LANE], even[:, LANE:] + odd[:, :LANE], odd[:, LANE:]], axis=1)
            lanes = pl.ds(pl.multiple_of((step * chunk + k) * PAIR_LANES, LANE), PAIR_LANES)
            out_ref[0, :, lanes] = potential * right_ref[0, :, lanes].astype(jnp.float32)
        return carry

    lax.fori_loop(0, half // chunk, depth_step, 0)


def fit_kernel(aux_ref, slots_ref, count_ref, tiles_ref, density_ref, gamma_ref, rows_ref):
    rows_ref[...] = density_ref[...].astype(jnp.float32)
    gamma_ref[...] = jnp.zeros_like(gamma_ref)
    base = lax.axis_index("pen") * gamma_ref.shape[0]
    for t in range(tiles_ref.shape[0]):
        row = jnp.broadcast_to(rows_ref[pl.ds(slots_ref[t], 1), :], (ROWS, LANE)).astype(jnp.bfloat16)
        value = lax.dot_general(row, tiles_ref[t], (((1,), (1,)), ((), ())), preferred_element_type=jnp.float32)
        place = pl.ds(aux_ref[t] - base, 1)
        gamma_ref[place, :] += jnp.where(t < count_ref[0], value[:1], 0.0)


def build_kernel(aux_ref, slots_ref, count_ref, tiles_ref, coef_ref, part_ref):
    part_ref[...] = jnp.zeros_like(part_ref)
    base = lax.axis_index("pen") * coef_ref.shape[0]
    for t in range(tiles_ref.shape[0]):
        row = jnp.broadcast_to(coef_ref[pl.ds(aux_ref[t] - base, 1), :], (ROWS, LANE)).astype(jnp.bfloat16)
        value = dot32(row, tiles_ref[t])
        place = pl.ds(slots_ref[t], 1)
        part_ref[place, :] += jnp.where(t < count_ref[0], value[:1], 0.0)


def tile_call(kernel, tiles, rows, out_rows, scratch, name):
    tile_blocks, tile_aux, tile_pair, tile_count = tiles
    return pl.pallas_call(
        kernel,
        out_shape=jax.ShapeDtypeStruct((out_rows, LANE), jnp.float32),
        grid_spec=pltpu.PrefetchScalarGridSpec(
            num_scalar_prefetch=3,
            grid=(1,),
            in_specs=[whole_spec(tile_blocks.shape), whole_spec(rows.shape)],
            out_specs=whole_spec((out_rows, LANE)),
            scratch_shapes=scratch,
        ),
        compiler_params=pltpu.CompilerParams(vmem_limit_bytes=TILE_VMEM_BYTES),
        cost_estimate=pl.CostEstimate(
            flops=2 * tile_blocks.size * ROWS, bytes_accessed=2 * tile_blocks.size, transcendentals=0
        ),
        name=name,
    )(tile_aux, tile_pair, tile_count, tile_blocks, rows)


def whole_spec(shape):
    return pl.BlockSpec(shape, lambda *_: (0,) * len(shape))


def column_scratch():
    return [
        pltpu.VMEM((2, (NG + 1) * ROWS, LANE), jnp.float32),
        pltpu.VMEM(((NG + 1) * ROWS, LANE), jnp.float32),
        pltpu.VMEM(((NG // 2 + 1) * ROWS, LANE), jnp.float32),
    ]


def forward_planes(pair_index, pair, orbitals, depth_tables, cols_table, pen, first, count, earlier, after):
    slab = NG // pen
    width = width_of(slab)
    skip = first // ROWS
    near = jax.ShapeDtypeStruct((slab, width), jnp.bfloat16)
    far = jax.ShapeDtypeStruct((count, width), jnp.bfloat16)
    operands = [pair_index, orbitals, orbitals, depth_tables, cols_table]
    aliases = {len(operands) + s: s for s in range(len(earlier))}
    operands += [*earlier, *after]
    return pl.pallas_call(
        functools.partial(forward_kernel, slab, pen),
        out_shape=[near] * NEAR + [far] * (pen - NEAR),
        grid_spec=pltpu.PrefetchScalarGridSpec(
            num_scalar_prefetch=1,
            grid=(count // ROWS,),
            in_specs=[
                pl.BlockSpec((1, ROWS, NG * NG), lambda b, pairs: (pairs[pair, 0], b + skip, 0)),
                pl.BlockSpec((1, ROWS, NG * NG), lambda b, pairs: (pairs[pair, 1], b + skip, 0)),
                whole_spec(depth_tables.shape),
                whole_spec(cols_table.shape),
            ]
            + [pl.BlockSpec(memory_space=pl.ANY)] * (len(earlier) + len(after)),
            out_specs=[pl.BlockSpec((ROWS, width), lambda b, *_: (b + skip, 0))] * NEAR
            + [pl.BlockSpec((ROWS, width), lambda b, *_: (b, 0))] * (pen - NEAR),
            scratch_shapes=column_scratch() + [pltpu.VMEM((NG + NG // 2, LANE), jnp.float32)],
        ),
        input_output_aliases=aliases,
        compiler_params=pltpu.CompilerParams(vmem_limit_bytes=VMEM_BYTES if earlier else VMEM_FIRST),
        cost_estimate=pl.CostEstimate(
            flops=2 * 6 * count * NG * NG * NG, bytes_accessed=6 * count * NG * NG, transcendentals=0
        ),
        name="forward_planes",
    )(*operands)


def middle_columns(fields, in_pieces, tables, grid_table, part, pen, out_pieces, extra):
    slab = NG // pen
    width = width_of(slab)
    block = width // 8
    out_shapes, out_specs = [], []
    for s, first, count in out_pieces:
        if extra and first + count == slab:
            out_shapes.append(jax.ShapeDtypeStruct((count, width + LANE), jnp.bfloat16))
            out_specs.append(whole_spec((count, width + LANE)))
        else:
            out_shapes.append(jax.ShapeDtypeStruct((count, width), jnp.bfloat16))
            out_specs.append(pl.BlockSpec((count, block), lambda b, *_: (0, b)))
    in_specs = [whole_spec(table.shape) for table in tables]
    in_specs += [pl.BlockSpec((grid_table.shape[0], block), lambda b, *_: (0, b)), whole_spec(part.shape)]
    in_specs += [pl.BlockSpec((count, block), lambda b, *_: (0, b)) for s, first, count in in_pieces]
    return pl.pallas_call(
        functools.partial(middle_kernel, pen, in_pieces, out_pieces, extra),
        out_shape=out_shapes,
        grid=(width // block,),
        in_specs=in_specs,
        out_specs=out_specs,
        scratch_shapes=[pltpu.VMEM((NG, block), jnp.bfloat16)],
        compiler_params=pltpu.CompilerParams(vmem_limit_bytes=VMEM_BYTES),
        cost_estimate=pl.CostEstimate(flops=2 * 5 * NG * NG * width, bytes_accessed=8 * NG * width, transcendentals=0),
        name="middle_columns",
    )(*tables, grid_table, part, *fields)


def inverse_planes(pair_index, pair, fields, orbitals, cols_table, depth_tables, first, earlier, part_rows):
    pen = len(fields)
    slab = NG // pen
    count = fields[-1].shape[0]
    skip = first // ROWS
    out_shapes = [jax.ShapeDtypeStruct((pair_index.shape[0], slab, NG * NG), jnp.float32)]
    out_specs = [pl.BlockSpec((1, ROWS, NG * NG), lambda b, *_: (pair, b + skip, 0))]
    if part_rows:
        out_shapes.append(jax.ShapeDtypeStruct((part_rows, LANE), jnp.float32))
        out_specs.append(whole_spec((part_rows, LANE)))
    in_specs = [pl.BlockSpec((ROWS, field.shape[1]), lambda b, *_: (b + skip, 0)) for field in fields[:NEAR]]
    in_specs += [pl.BlockSpec((ROWS, field.shape[1]), lambda b, *_: (b, 0)) for field in fields[NEAR:]]
    in_specs += [
        pl.BlockSpec((1, ROWS, NG * NG), lambda b, pairs: (pairs[pair, 1], b + skip, 0)),
        whole_spec(cols_table.shape),
        whole_spec(depth_tables.shape),
    ]
    operands = [pair_index, *fields, orbitals, cols_table, depth_tables]
    aliases = {}
    if earlier is not None:
        aliases = {len(operands): 0}
        in_specs.append(pl.BlockSpec(memory_space=pl.ANY))
        operands.append(earlier)
    return pl.pallas_call(
        functools.partial(inverse_kernel, slab, pen, bool(part_rows)),
        out_shape=out_shapes,
        grid_spec=pltpu.PrefetchScalarGridSpec(
            num_scalar_prefetch=1,
            grid=(count // ROWS,),
            in_specs=in_specs,
            out_specs=out_specs,
            scratch_shapes=column_scratch(),
        ),
        input_output_aliases=aliases,
        compiler_params=pltpu.CompilerParams(vmem_limit_bytes=VMEM_BYTES),
        cost_estimate=pl.CostEstimate(
            flops=2 * 5 * count * NG * NG * NG, bytes_accessed=8 * count * NG * NG, transcendentals=0
        ),
        name="inverse_planes",
    )(*operands)


def exchange(s, field, pen):
    return lax.ppermute(field, "pen", [(i, i ^ s) for i in range(pen)]) if s else field


def stack_split(table):
    return np.concatenate(split_table(table), axis=0)


def depth_table_set():
    lanes = np.arange(2 * LANE)
    freq = np.where(lanes < NG, lanes, lanes - TAIL)
    tables = []
    for parity in range(2):
        depth = lanes - parity * TAIL
        inside = (depth >= 0) & (depth < NG)
        tables.append(np.where(inside[:, None], cas_table(depth[:, None], freq[None, :]), 0.0))
    return np.stack(split_table(np.stack(tables)), axis=1)


def grid_weights(me, slab):
    lane = jnp.arange(LANE, dtype=jnp.int32)[None, :]
    row = jnp.arange(slab, dtype=jnp.int32)[:, None]
    head_col, head_depth = jnp.broadcast_arrays(row, lane)
    tail_row = row[: slab // 2]
    tail_col = jnp.where(lane < TAIL, tail_row, tail_row + slab // 2)
    tail_depth = jnp.broadcast_to(LANE + lane % TAIL, tail_col.shape)
    col = signed_freq(me * slab + jnp.concatenate([head_col, tail_col], axis=0).reshape(-1), NG)
    depth = signed_freq(jnp.concatenate([head_depth, tail_depth], axis=0).reshape(-1), NG)
    plane = jnp.arange(NG // 2 + ROWS // 2, dtype=jnp.int32)
    square_sum = (plane * plane)[:, None] + (col * col + depth * depth)[None, :]
    return coulomb_kernel(square_sum, NG) / float(NG * NG * NG)


def plane_frequencies():
    upper = (NG - np.arange(NG // 2)) % NG
    upper[0] = NG // 2
    return np.concatenate([np.arange(NG // 2), upper])


def plane_runs(slab, first, last):
    if slab > ROWS and first:
        return ((0, ROWS), (ROWS, slab - ROWS))
    if slab > ROWS and last:
        return ((0, slab - ROWS), (slab - ROWS, ROWS))
    return ((0, slab),)


def pieces_of(pen, runs):
    far = tuple((s, first, count) for first, count in runs for s in range(pen - 1, NEAR - 1, -1))
    return far + tuple((s, 0, NG // pen) for s in range(NEAR - 1, -1, -1))


def both_parts(orbitals, pair_index, pen, coulomb_local, coulomb_part):
    slab = NG // pen
    pairs = pair_index.shape[0]
    me = lax.axis_index("pen").astype(jnp.int32)
    positions = np.arange(NG)
    interleaved = np.concatenate([positions[0::2], positions[1::2]])
    depth_np = depth_table_set()
    depth_tables, depth_back = jnp.asarray(depth_np), jnp.asarray(np.swapaxes(depth_np, 2, 3))
    cols_forward = jnp.asarray(stack_split(cas_table(positions[:, None], interleaved[None, :])))
    cols_back = jnp.asarray(stack_split(cas_table(interleaved[:, None], positions[None, :])))
    frequencies = plane_frequencies()
    plane_tables = (
        jnp.asarray(stack_split(cas_table(frequencies[:, None], positions[None, :]))),
        jnp.asarray(stack_split(cas_table(positions[:, None], frequencies[None, :]))),
    )

    held, after = [], []
    for p in range(pairs):
        runs = plane_runs(slab, p == 0, False)
        taken, made = {}, ()
        for first, count in runs:
            made = forward_planes(
                pair_index, p, orbitals, depth_tables, cols_forward, pen, first, count, made[:NEAR], after if first == 0 else ()
            )
            for s in range(NEAR, pen):
                taken[s, first] = exchange(s, made[s], pen)
            if p == 0 and first == 0:
                local = coulomb_local(made[-1])
        for s in range(NEAR):
            taken[s, 0] = exchange(s, made[s], pen)
        pieces = pieces_of(pen, runs)
        held.append((pieces, [taken[s, first] for s, first, count in pieces]))
        if p == 0:
            late_me, _ = lax.optimization_barrier((me, made[-1]))
            grid_table = grid_weights(late_me, slab)
            after = [grid_table, local]
    part = coulomb_part(local)

    back = []
    for p in range(pairs):
        last = p == pairs - 1
        fed = part if last else jnp.zeros_like(part)
        runs = plane_runs(slab, False, last)
        pieces = pieces_of(pen, runs)
        filtered = middle_columns(held[p][1], held[p][0], plane_tables, grid_table, fed, pen, pieces, last)
        back.append((runs, {piece[:2]: exchange(piece[0], field, pen) for piece, field in zip(pieces, filtered)}))

    terms = None
    for p in range(pairs):
        runs, taken = back[p]
        for first, count in runs:
            final = p == pairs - 1 and first + count == slab
            fields = [taken[s, 0 if s < NEAR else first] for s in range(pen)]
            made = inverse_planes(
                pair_index, p, fields, orbitals, cols_back, depth_back, first, terms, part.shape[1] if final else 0
            )
            terms = made[0]
    return made[1], terms


def pair_fields_plain(orbitals, pair_index, pen):
    slab = NG // pen
    plane_rows = orbitals.shape[1]
    positions = jnp.arange(NG, dtype=jnp.int32)
    places = np.arange(NG)
    high, low = (jnp.asarray(part) for part in split_table(cas_table(places[:, None], places[None, :])))

    def transform(axes, field):
        first = lax.reduce_precision(field, 8, 7)
        second = (field - first).astype(jnp.bfloat16)
        first = first.astype(jnp.bfloat16)
        return (
            jnp.einsum(axes, first, high, preferred_element_type=jnp.float32)
            + jnp.einsum(axes, first, low, preferred_element_type=jnp.float32)
            + jnp.einsum(axes, second, high, preferred_element_type=jnp.float32)
        )

    grid = orbitals.reshape(orbitals.shape[0], plane_rows, NG, NG)
    right = grid[pair_index[:, 1]].astype(jnp.float32)
    field = grid[pair_index[:, 0]].astype(jnp.float32) * right
    field = transform("pxyk,yv->pxvk", transform("pxyz,zk->pxyk", field))
    field = lax.all_to_all(field.astype(jnp.bfloat16), "pen", split_axis=2, concat_axis=1, tiled=True)
    col = signed_freq(lax.axis_index("pen") * slab + jnp.arange(slab, dtype=jnp.int32), NG)
    freq = signed_freq(positions, NG)
    square_sum = (freq * freq)[:, None, None] + (col * col)[None, :, None] + (freq * freq)[None, None, :]
    weights = coulomb_kernel(square_sum, NG) / float(NG * NG * NG)
    field = transform("pxyk,xv->pvyk", field.astype(jnp.float32)) * weights[None]
    field = transform("pxyk,xv->pvyk", field).astype(jnp.bfloat16)
    field = lax.all_to_all(field, "pen", split_axis=1, concat_axis=2, tiled=True)
    field = transform("pxyk,yv->pxvk", field.astype(jnp.float32))
    terms = transform("pxyk,kz->pxyz", field) * right
    return terms.reshape(terms.shape[0], plane_rows, NG * NG)


def tile_pass(tile_blocks, aux_local, pair_ids, live_count, contribute, initial):
    step_rows = 8

    def add_block(step_index, running):
        first_slot = step_index * step_rows
        tile_block = lax.dynamic_slice_in_dim(tile_blocks, first_slot, step_rows, 0)
        aux_block = lax.dynamic_slice_in_dim(aux_local, first_slot, step_rows, 0)
        pair_block = lax.dynamic_slice_in_dim(pair_ids, first_slot, step_rows, 0)
        slot_ids = first_slot + jnp.arange(step_rows, dtype=jnp.int32)
        live_mask = (slot_ids < live_count).astype(jnp.float32)
        return contribute(running, tile_block, aux_block, pair_block, live_mask)

    block_count = (live_count + step_rows - 1) // step_rows
    return lax.fori_loop(0, block_count, add_block, initial)


def to_all(values, count, axes):
    copies = jnp.broadcast_to(values[None], (count, *values.shape))
    return lax.all_to_all(copies, axes, split_axis=0, concat_axis=0, tiled=True)


def coulomb_partial(tile_blocks, tile_aux, tile_pair, tile_count, density, metric_inv):
    aux_count = metric_inv.shape[0]
    dens_all = lax.all_gather(density, "blk", axis=0, tiled=True)
    aux_local = tile_aux - lax.axis_index("pen") * aux_count
    live_count = tile_count[0]
    aux_ids = jnp.arange(aux_count, dtype=jnp.int32)

    def add_fit(running, tile_block, aux_block, pair_block, live_mask):
        dens_rows = dens_all[pair_block]
        partial_value = jnp.einsum("tap,tp->ta", tile_block, dens_rows, preferred_element_type=jnp.float32)
        partial_value = partial_value * live_mask[:, None]
        selector = (aux_block[:, None] == aux_ids[None, :]).astype(jnp.float32)
        return running + jnp.einsum("tk,ta->ka", selector, partial_value, precision=PRECISE)

    gamma = jnp.zeros((aux_count, tile_blocks.shape[1]), jnp.float32)
    gamma = tile_pass(tile_blocks, aux_local, tile_pair, live_count, add_fit, gamma)
    gamma_all = lax.psum(gamma, ("grp", "blk"))
    coef = jnp.einsum("kab,kb->ka", metric_inv, gamma_all, precision=PRECISE).astype(jnp.bfloat16)

    def add_coulomb(running, tile_block, aux_block, pair_block, live_mask):
        selector = (aux_block[:, None] == aux_ids[None, :]).astype(jnp.bfloat16)
        coef_rows = jnp.dot(selector, coef, preferred_element_type=jnp.float32).astype(jnp.bfloat16)
        partial_value = jnp.einsum("tap,ta->tp", tile_block, coef_rows, preferred_element_type=jnp.float32)
        partial_value = partial_value * live_mask[:, None]
        return running.at[pair_block].add(partial_value)

    part = jnp.zeros((dens_all.shape[0], tile_blocks.shape[2]), jnp.float32)
    return tile_pass(tile_blocks, aux_local, tile_pair, live_count, add_coulomb, part)


def body(tile_blocks, tile_aux, tile_pair, tile_count, density, metric_inv, orbitals, pair_index):
    pen, blk, grp = (lax.axis_size(name) for name in ("pen", "blk", "grp"))
    slab = orbitals.shape[1]
    rows = density.shape[0] // (grp * pen)
    tiles = (tile_blocks, tile_aux, tile_pair, tile_count)
    if slab % ROWS == 0 and pen & (pen - 1) == 0 and pen >= NEAR and rows <= ROWS // 3:

        def coulomb_local(after):
            late_density, _ = lax.optimization_barrier((density, after))
            dens_all = to_all(late_density, blk, "blk").reshape(-1, LANE)
            scratch = [pltpu.VMEM(dens_all.shape, jnp.float32)]
            gamma = tile_call(fit_kernel, tiles, dens_all, metric_inv.shape[0], scratch, "fit_tiles")
            gamma = to_all(gamma, grp * blk, ("grp", "blk")).sum(axis=0)
            coef = jnp.einsum("kab,kb->ka", metric_inv, gamma, precision=PRECISE)
            coef = lax.reduce_precision(coef, 8, 7)
            return tile_call(build_kernel, tiles, coef, dens_all.shape[0], [], "build_tiles")

        def coulomb_part(local):
            shares = local.reshape(grp, pen, blk, rows, LANE).transpose(0, 2, 1, 3, 4)
            shares = shares.reshape(grp * blk, pen * rows, LANE)
            taken = lax.all_to_all(shares, ("grp", "blk"), split_axis=0, concat_axis=0, tiled=True)
            return taken.sum(axis=0).reshape(pen, rows, LANE)

        return both_parts(orbitals, pair_index, pen, coulomb_local, coulomb_part)
    part = coulomb_partial(*tiles, density, metric_inv)
    coulomb = lax.psum_scatter(part, ("grp", "pen", "blk"), scatter_dimension=0, tiled=True)
    return coulomb, pair_fields_plain(orbitals, pair_index, pen)


def solution(mesh):
    placed = (
        P(("grp", "pen", "blk"), None, None),
        P(("grp", "pen", "blk")),
        P(("grp", "pen", "blk")),
        P(("grp", "pen", "blk")),
        P("blk", None),
        P("pen", None, None),
        P(None, "pen", None),
        P(("grp", "blk"), None),
    )
    return jax.shard_map(
        body,
        mesh=mesh,
        in_specs=placed,
        out_specs=(P(("grp", "pen", "blk"), None), P(("grp", "blk"), "pen", None)),
        check_vma=False,
    )
```

```python
import functools
import math

import jax
import jax.numpy as jnp
import ml_dtypes
import numpy as np
from jax import lax
from jax.experimental import pallas as pl
from jax.experimental.pallas import tpu as pltpu
from jax.sharding import PartitionSpec as P

NG = 192
LANE = 128
TAIL = NG - LANE
PAIR_LANES = 2 * NG
ROWS = 16
NEAR = 2
UNROLL = 8

PRECISE = lax.Precision.HIGHEST
SPACING = 0.1348
VMEM_BYTES = 32 * 1024 * 1024
TILE_VMEM_BYTES = 16 * 1024 * 1024
VMEM_FIRST = 56 * 1024 * 1024


def signed_freq(position, length):
    return jnp.where(position < length // 2, position, position - length)


def coulomb_kernel(square_sum, length):
    box_length = SPACING * length
    kernel_scale = box_length * box_length / math.pi
    squares = square_sum.astype(jnp.float32)
    magnitude = jnp.sqrt(squares)
    denominator = jnp.where(square_sum == 0, 1.0, squares)
    regular = kernel_scale * (1.0 - jnp.cos(math.pi * magnitude)) / denominator
    return jnp.where(square_sum == 0, kernel_scale * math.pi * math.pi / 2.0, regular)


def cas_table(left, right):
    angles = (left * right % NG) * (2.0 * math.pi / NG)
    return np.cos(angles) + np.sin(angles)


def split_table(table):
    high = table.astype(ml_dtypes.bfloat16)
    return high, (table - high.astype(np.float64)).astype(ml_dtypes.bfloat16)


def split(values):
    high = values.astype(jnp.bfloat16)
    low = (values - high.astype(jnp.float32)).astype(jnp.bfloat16)
    return high, low


def split_rest(values):
    high = values.astype(jnp.bfloat16).astype(jnp.float32)
    return high, values - high


def width_of(slab):
    return slab * NG


def dot32(left, right):
    return jnp.dot(left, right, preferred_element_type=jnp.float32)


def split_dot(values, high_weight, low_weight):
    high, low = split(values)
    return dot32(high, high_weight) + dot32(high, low_weight) + dot32(low, high_weight)


def stacked_dot(stacked, values):
    count = stacked.shape[0] // 2
    high, low = split(values)
    both = dot32(stacked, high)
    return both[:count] + both[count:] + dot32(stacked[:count], low)


def stacked_dot_exact(stacked, values):
    count = stacked.shape[0] // 2
    both = dot32(stacked, values)
    return both[:count] + both[count:]


def forward_kernel(slab, pen, pairs_ref, left_ref, right_ref, depth_ref, cols_ref, *refs):
    outs, (rows_ref, head_ref, tail_ref, rest_ref) = refs[-4 - pen : -4], refs[-4:]
    half = NG // 2
    chunk = 32

    def depth_step(step, carry):
        start = pl.multiple_of(step * (chunk * PAIR_LANES), LANE)
        lanes = pl.ds(start, chunk * PAIR_LANES)
        field = left_ref[0, :, lanes].astype(jnp.float32) * right_ref[0, :, lanes].astype(jnp.float32)
        high, low = split(field)
        for parity in range(2):
            parts = []
            for source in (high, low):
                first = parity * LANE
                parts.append(
                    jnp.concatenate(
                        [source[:, k * PAIR_LANES + first : k * PAIR_LANES + first + 2 * LANE] for k in range(chunk)], axis=0
                    )
                )
            table_high, table_low = depth_ref[parity, 0], depth_ref[parity, 1]
            result = dot32(parts[0], table_high) + dot32(parts[0], table_low) + dot32(parts[1], table_high)
            place = pl.ds(pl.multiple_of((parity * half + step * chunk) * ROWS, ROWS), chunk * ROWS)
            rows_ref[0, place, :] = result[:, :LANE]
            rows_ref[1, place, :] = result[:, LANE:]
        return carry

    lax.fori_loop(0, half // chunk, depth_step, 0)
    low_lanes = lax.broadcasted_iota(jnp.int32, (slab // 2, LANE), 1) < TAIL

    @pl.when(pl.program_id(0) == 0)
    def _():
        rest_ref[...] = jnp.zeros_like(rest_ref)

    def rounded(values, place):
        values = values + rest_ref[place, :]
        kept = values.astype(jnp.bfloat16).astype(jnp.float32)
        rest_ref[place, :] = values - kept
        return kept

    def cols_step(plane, carry):
        strided = pl.ds(plane, NG, stride=ROWS)
        field = jnp.concatenate([rows_ref[0, strided, :], rows_ref[1, strided, :]], axis=1)
        result = stacked_dot(cols_ref[...], field)
        head_ref[strided, :] = rounded(result[:, :LANE], pl.ds(0, NG))
        tails = []
        for q in range(pen):
            first = result[q * slab : q * slab + slab // 2, LANE:]
            second = result[q * slab + slab // 2 : (q + 1) * slab, LANE:]
            tails.append(jnp.where(low_lanes, first, second))
        tail_ref[pl.ds(plane, half, stride=ROWS), :] = rounded(jnp.concatenate(tails, axis=0), pl.ds(NG, half))
        return carry

    lax.fori_loop(0, ROWS, cols_step, 0, unroll=UNROLL)
    for s in range(pen):
        owner = lax.axis_index("pen") ^ s
        for r in range(slab):
            place = pl.ds(pl.multiple_of((owner * slab + r) * ROWS, ROWS), ROWS)
            outs[s][:, r * LANE : (r + 1) * LANE] = head_ref[place, :].astype(jnp.bfloat16)
        for r in range(slab // 2):
            place = pl.ds(pl.multiple_of((owner * (slab // 2) + r) * ROWS, ROWS), ROWS)
            outs[s][:, (slab + r) * LANE : (slab + r + 1) * LANE] = tail_ref[place, :].astype(jnp.bfloat16)


def middle_kernel(pen, in_pieces, out_pieces, extra, in_ref, out_table_ref, grid_ref, part_ref, *refs):
    fields, outs, planes_ref = refs[: len(in_pieces)], refs[len(in_pieces) : -1], refs[-1]
    slab = NG // pen
    block = planes_ref.shape[1]

    def place(s, first, count):
        return pl.ds(pl.multiple_of((lax.axis_index("pen") ^ s) * slab + first, ROWS), count)

    for field, piece in zip(fields, in_pieces):
        planes_ref[place(*piece), :] = field[...]
    half = NG // 2
    weights = grid_ref[:half, :]
    top = lax.broadcasted_iota(jnp.int32, (ROWS // 2, block), 0) == 0
    mirrored = jnp.where(top, grid_ref[half:, :], weights[: ROWS // 2])
    weights = jnp.concatenate([weights, mirrored, weights[ROWS // 2 :]], axis=0)
    spectral = stacked_dot_exact(in_ref[...], planes_ref[...]) * weights
    planes_ref[...] = stacked_dot(out_table_ref[...], spectral).astype(jnp.bfloat16)
    for out_ref, piece in zip(outs, out_pieces):
        values = planes_ref[place(*piece), :]
        if not (extra and piece[1] + piece[2] == slab):
            out_ref[...] = values
            continue
        lanes = pl.ds(pl.multiple_of(pl.program_id(0) * block, LANE), block)
        out_ref[:, lanes] = values
        high, rest = split_rest(part_ref[lax.axis_index("pen") ^ piece[0]])
        middle, rest = split_rest(rest)
        blank = jnp.zeros((ROWS - 3 * high.shape[0], LANE), jnp.float32)
        if piece[2] > ROWS:
            out_ref[: piece[2] - ROWS, width_of(slab) :] = jnp.zeros((piece[2] - ROWS, LANE), jnp.bfloat16)
        tag = jnp.concatenate([high, middle, rest, blank], axis=0).astype(jnp.bfloat16)
        out_ref[piece[2] - ROWS :, width_of(slab) :] = tag


def inverse_kernel(slab, pen, extra, pairs_ref, *refs):
    fields = refs[:pen]
    right_ref, cols_ref, depth_ref = refs[pen : pen + 3]
    out_ref, rows_ref, head_ref, tail_ref = refs[-4:]
    if extra:
        part_ref, out_ref = refs[-4], refs[-5]
        rows = part_ref.shape[0]
        tags = [field[:, width_of(slab) :].astype(jnp.float32) for field in fields]
        part_ref[...] = sum(tag[c * rows : (c + 1) * rows] for c in (2, 1, 0) for tag in tags)
    half = NG // 2
    chunk = 32
    for s in range(pen):
        owner = lax.axis_index("pen") ^ s
        for r in range(slab):
            place = pl.ds(pl.multiple_of((owner * slab + r) * ROWS, ROWS), ROWS)
            head_ref[place, :] = fields[s][:, r * LANE : (r + 1) * LANE].astype(jnp.float32)
        for r in range(slab // 2):
            place = pl.ds(pl.multiple_of((owner * (slab // 2) + r) * ROWS, ROWS), ROWS)
            tail_ref[place, :] = fields[s][:, (slab + r) * LANE : (slab + r + 1) * LANE].astype(jnp.float32)
    low_lanes = lax.broadcasted_iota(jnp.int32, (slab // 2, LANE), 1) < TAIL

    def cols_step(plane, carry):
        strided = pl.ds(plane, NG, stride=ROWS)
        tail = tail_ref[pl.ds(plane, half, stride=ROWS), :]
        pieces = []
        for q in range(pen):
            both = tail[q * (slab // 2) : (q + 1) * (slab // 2)]
            pieces.append(jnp.where(low_lanes, both, 0.0))
            pieces.append(jnp.where(low_lanes, 0.0, both))
        field = jnp.concatenate([head_ref[strided, :], jnp.concatenate(pieces, axis=0)], axis=1)
        result = stacked_dot_exact(cols_ref[...], field.astype(jnp.bfloat16))
        rows_ref[0, strided, :] = result[:, :LANE]
        rows_ref[1, strided, :] = result[:, LANE:]
        return carry

    lax.fori_loop(0, ROWS, cols_step, 0, unroll=UNROLL)

    def depth_step(step, carry):
        results = []
        for parity in range(2):
            place = pl.ds(pl.multiple_of((parity * half + step * chunk) * ROWS, ROWS), chunk * ROWS)
            field = jnp.concatenate([rows_ref[0, place, :], rows_ref[1, place, :]], axis=1)
            results.append(split_dot(field, depth_ref[parity, 0], depth_ref[parity, 1]))
        for k in range(chunk):
            even, odd = (value[k * ROWS : (k + 1) * ROWS] for value in results)
            potential = jnp.concatenate([even[:, :LANE], even[:, LANE:] + odd[:, :LANE], odd[:, LANE:]], axis=1)
            lanes = pl.ds(pl.multiple_of((step * chunk + k) * PAIR_LANES, LANE), PAIR_LANES)
            out_ref[0, :, lanes] = potential * right_ref[0, :, lanes].astype(jnp.float32)
        return carry

    lax.fori_loop(0, half // chunk, depth_step, 0)


def fit_kernel(aux_ref, slots_ref, count_ref, tiles_ref, density_ref, gamma_ref, rows_ref):
    rows_ref[...] = density_ref[...].astype(jnp.float32)
    gamma_ref[...] = jnp.zeros_like(gamma_ref)
    base = lax.axis_index("pen") * gamma_ref.shape[0]
    for t in range(tiles_ref.shape[0]):
        row = jnp.broadcast_to(rows_ref[pl.ds(slots_ref[t], 1), :], (ROWS, LANE)).astype(jnp.bfloat16)
        value = lax.dot_general(row, tiles_ref[t], (((1,), (1,)), ((), ())), preferred_element_type=jnp.float32)
        place = pl.ds(aux_ref[t] - base, 1)
        gamma_ref[place, :] += jnp.where(t < count_ref[0], value[:1], 0.0)


def build_kernel(aux_ref, slots_ref, count_ref, tiles_ref, coef_ref, part_ref):
    part_ref[...] = jnp.zeros_like(part_ref)
    base = lax.axis_index("pen") * coef_ref.shape[0]
    for t in range(tiles_ref.shape[0]):
        row = jnp.broadcast_to(coef_ref[pl.ds(aux_ref[t] - base, 1), :], (ROWS, LANE)).astype(jnp.bfloat16)
        value = dot32(row, tiles_ref[t])
        place = pl.ds(slots_ref[t], 1)
        part_ref[place, :] += jnp.where(t < count_ref[0], value[:1], 0.0)


def tile_call(kernel, tiles, rows, out_rows, scratch, name):
    tile_blocks, tile_aux, tile_pair, tile_count = tiles
    return pl.pallas_call(
        kernel,
        out_shape=jax.ShapeDtypeStruct((out_rows, LANE), jnp.float32),
        grid_spec=pltpu.PrefetchScalarGridSpec(
            num_scalar_prefetch=3,
            grid=(1,),
            in_specs=[whole_spec(tile_blocks.shape), whole_spec(rows.shape)],
            out_specs=whole_spec((out_rows, LANE)),
            scratch_shapes=scratch,
        ),
        compiler_params=pltpu.CompilerParams(vmem_limit_bytes=TILE_VMEM_BYTES),
        cost_estimate=pl.CostEstimate(
            flops=2 * tile_blocks.size * ROWS, bytes_accessed=2 * tile_blocks.size, transcendentals=0
        ),
        name=name,
    )(tile_aux, tile_pair, tile_count, tile_blocks, rows)


def whole_spec(shape):
    return pl.BlockSpec(shape, lambda *_: (0,) * len(shape))


def column_scratch():
    return [
        pltpu.VMEM((2, (NG + 1) * ROWS, LANE), jnp.float32),
        pltpu.VMEM(((NG + 1) * ROWS, LANE), jnp.float32),
        pltpu.VMEM(((NG // 2 + 1) * ROWS, LANE), jnp.float32),
    ]


def forward_planes(pair_index, pair, orbitals, depth_tables, cols_table, pen, first, count, earlier, after):
    slab = NG // pen
    width = width_of(slab)
    skip = first // ROWS
    near = jax.ShapeDtypeStruct((slab, width), jnp.bfloat16)
    far = jax.ShapeDtypeStruct((count, width), jnp.bfloat16)
    operands = [pair_index, orbitals, orbitals, depth_tables, cols_table]
    aliases = {len(operands) + s: s for s in range(len(earlier))}
    operands += [*earlier, *after]
    return pl.pallas_call(
        functools.partial(forward_kernel, slab, pen),
        out_shape=[near] * NEAR + [far] * (pen - NEAR),
        grid_spec=pltpu.PrefetchScalarGridSpec(
            num_scalar_prefetch=1,
            grid=(count // ROWS,),
            in_specs=[
                pl.BlockSpec((1, ROWS, NG * NG), lambda b, pairs: (pairs[pair, 0], b + skip, 0)),
                pl.BlockSpec((1, ROWS, NG * NG), lambda b, pairs: (pairs[pair, 1], b + skip, 0)),
                whole_spec(depth_tables.shape),
                whole_spec(cols_table.shape),
            ]
            + [pl.BlockSpec(memory_space=pl.ANY)] * (len(earlier) + len(after)),
            out_specs=[pl.BlockSpec((ROWS, width), lambda b, *_: (b + skip, 0))] * NEAR
            + [pl.BlockSpec((ROWS, width), lambda b, *_: (b, 0))] * (pen - NEAR),
            scratch_shapes=column_scratch() + [pltpu.VMEM((NG + NG // 2, LANE), jnp.float32)],
        ),
        input_output_aliases=aliases,
        compiler_params=pltpu.CompilerParams(vmem_limit_bytes=VMEM_BYTES if earlier else VMEM_FIRST),
        cost_estimate=pl.CostEstimate(
            flops=2 * 6 * count * NG * NG * NG, bytes_accessed=6 * count * NG * NG, transcendentals=0
        ),
        name="forward_planes",
    )(*operands)


def middle_columns(fields, in_pieces, tables, grid_table, part, pen, out_pieces, extra):
    slab = NG // pen
    width = width_of(slab)
    block = width // 8
    out_shapes, out_specs = [], []
    for s, first, count in out_pieces:
        if extra and first + count == slab:
            out_shapes.append(jax.ShapeDtypeStruct((count, width + LANE), jnp.bfloat16))
            out_specs.append(whole_spec((count, width + LANE)))
        else:
            out_shapes.append(jax.ShapeDtypeStruct((count, width), jnp.bfloat16))
            out_specs.append(pl.BlockSpec((count, block), lambda b, *_: (0, b)))
    in_specs = [whole_spec(table.shape) for table in tables]
    in_specs += [pl.BlockSpec((grid_table.shape[0], block), lambda b, *_: (0, b)), whole_spec(part.shape)]
    in_specs += [pl.BlockSpec((count, block), lambda b, *_: (0, b)) for s, first, count in in_pieces]
    return pl.pallas_call(
        functools.partial(middle_kernel, pen, in_pieces, out_pieces, extra),
        out_shape=out_shapes,
        grid=(width // block,),
        in_specs=in_specs,
        out_specs=out_specs,
        scratch_shapes=[pltpu.VMEM((NG, block), jnp.bfloat16)],
        compiler_params=pltpu.CompilerParams(vmem_limit_bytes=VMEM_BYTES),
        cost_estimate=pl.CostEstimate(flops=2 * 5 * NG * NG * width, bytes_accessed=8 * NG * width, transcendentals=0),
        name="middle_columns",
    )(*tables, grid_table, part, *fields)


def inverse_planes(pair_index, pair, fields, orbitals, cols_table, depth_tables, first, earlier, part_rows):
    pen = len(fields)
    slab = NG // pen
    count = fields[-1].shape[0]
    skip = first // ROWS
    out_shapes = [jax.ShapeDtypeStruct((pair_index.shape[0], slab, NG * NG), jnp.float32)]
    out_specs = [pl.BlockSpec((1, ROWS, NG * NG), lambda b, *_: (pair, b + skip, 0))]
    if part_rows:
        out_shapes.append(jax.ShapeDtypeStruct((part_rows, LANE), jnp.float32))
        out_specs.append(whole_spec((part_rows, LANE)))
    in_specs = [pl.BlockSpec((ROWS, field.shape[1]), lambda b, *_: (b + skip, 0)) for field in fields[:NEAR]]
    in_specs += [pl.BlockSpec((ROWS, field.shape[1]), lambda b, *_: (b, 0)) for field in fields[NEAR:]]
    in_specs += [
        pl.BlockSpec((1, ROWS, NG * NG), lambda b, pairs: (pairs[pair, 1], b + skip, 0)),
        whole_spec(cols_table.shape),
        whole_spec(depth_tables.shape),
    ]
    operands = [pair_index, *fields, orbitals, cols_table, depth_tables]
    aliases = {}
    if earlier is not None:
        aliases = {len(operands): 0}
        in_specs.append(pl.BlockSpec(memory_space=pl.ANY))
        operands.append(earlier)
    return pl.pallas_call(
        functools.partial(inverse_kernel, slab, pen, bool(part_rows)),
        out_shape=out_shapes,
        grid_spec=pltpu.PrefetchScalarGridSpec(
            num_scalar_prefetch=1,
            grid=(count // ROWS,),
            in_specs=in_specs,
            out_specs=out_specs,
            scratch_shapes=column_scratch(),
        ),
        input_output_aliases=aliases,
        compiler_params=pltpu.CompilerParams(vmem_limit_bytes=VMEM_BYTES),
        cost_estimate=pl.CostEstimate(
            flops=2 * 5 * count * NG * NG * NG, bytes_accessed=8 * count * NG * NG, transcendentals=0
        ),
        name="inverse_planes",
    )(*operands)


def exchange(s, field, pen):
    return lax.ppermute(field, "pen", [(i, i ^ s) for i in range(pen)]) if s else field


def stack_split(table):
    return np.concatenate(split_table(table), axis=0)


def depth_table_set():
    lanes = np.arange(2 * LANE)
    freq = np.where(lanes < NG, lanes, lanes - TAIL)
    tables = []
    for parity in range(2):
        depth = lanes - parity * TAIL
        inside = (depth >= 0) & (depth < NG)
        tables.append(np.where(inside[:, None], cas_table(depth[:, None], freq[None, :]), 0.0))
    return np.stack(split_table(np.stack(tables)), axis=1)


def grid_weights(me, slab):
    lane = jnp.arange(LANE, dtype=jnp.int32)[None, :]
    row = jnp.arange(slab, dtype=jnp.int32)[:, None]
    head_col, head_depth = jnp.broadcast_arrays(row, lane)
    tail_row = row[: slab // 2]
    tail_col = jnp.where(lane < TAIL, tail_row, tail_row + slab // 2)
    tail_depth = jnp.broadcast_to(LANE + lane % TAIL, tail_col.shape)
    col = signed_freq(me * slab + jnp.concatenate([head_col, tail_col], axis=0).reshape(-1), NG)
    depth = signed_freq(jnp.concatenate([head_depth, tail_depth], axis=0).reshape(-1), NG)
    plane = jnp.arange(NG // 2 + ROWS // 2, dtype=jnp.int32)
    square_sum = (plane * plane)[:, None] + (col * col + depth * depth)[None, :]
    return coulomb_kernel(square_sum, NG) / float(NG * NG * NG)


def plane_frequencies():
    upper = (NG - np.arange(NG // 2)) % NG
    upper[0] = NG // 2
    return np.concatenate([np.arange(NG // 2), upper])


def plane_runs(slab, first, last):
    if slab > ROWS and first:
        return ((0, ROWS), (ROWS, slab - ROWS))
    if slab > ROWS and last:
        return ((0, slab - ROWS), (slab - ROWS, ROWS))
    return ((0, slab),)


def pieces_of(pen, runs):
    far = tuple((s, first, count) for first, count in runs for s in range(pen - 1, NEAR - 1, -1))
    return far + tuple((s, 0, NG // pen) for s in range(NEAR - 1, -1, -1))


def both_parts(orbitals, pair_index, pen, coulomb_local, coulomb_part):
    slab = NG // pen
    pairs = pair_index.shape[0]
    me = lax.axis_index("pen").astype(jnp.int32)
    positions = np.arange(NG)
    interleaved = np.concatenate([positions[0::2], positions[1::2]])
    depth_np = depth_table_set()
    depth_tables, depth_back = jnp.asarray(depth_np), jnp.asarray(np.swapaxes(depth_np, 2, 3))
    cols_forward = jnp.asarray(stack_split(cas_table(positions[:, None], interleaved[None, :])))
    cols_back = jnp.asarray(stack_split(cas_table(interleaved[:, None], positions[None, :])))
    frequencies = plane_frequencies()
    plane_tables = (
        jnp.asarray(stack_split(cas_table(frequencies[:, None], positions[None, :]))),
        jnp.asarray(stack_split(cas_table(positions[:, None], frequencies[None, :]))),
    )

    held, after = [], []
    for p in range(pairs):
        runs = plane_runs(slab, p == 0, False)
        taken, made = {}, ()
        for first, count in runs:
            made = forward_planes(
                pair_index, p, orbitals, depth_tables, cols_forward, pen, first, count, made[:NEAR], after if first == 0 else ()
            )
            for s in range(NEAR, pen):
                taken[s, first] = exchange(s, made[s], pen)
            if p == 0 and first + count == slab:
                local = coulomb_local(made[-1])
        for s in range(NEAR):
            taken[s, 0] = exchange(s, made[s], pen)
        pieces = pieces_of(pen, runs)
        held.append((pieces, [taken[s, first] for s, first, count in pieces]))
        if p == 0:
            late_me, _ = lax.optimization_barrier((me, made[-1]))
            grid_table = grid_weights(late_me, slab)
            after = [grid_table, local]
    part = coulomb_part(local)

    back = []
    for p in range(pairs):
        last = p == pairs - 1
        fed = part if last else jnp.zeros_like(part)
        runs = plane_runs(slab, False, last)
        pieces = pieces_of(pen, runs)
        filtered = middle_columns(held[p][1], held[p][0], plane_tables, grid_table, fed, pen, pieces, last)
        back.append((runs, {piece[:2]: exchange(piece[0], field, pen) for piece, field in zip(pieces, filtered)}))

    terms = None
    for p in range(pairs):
        runs, taken = back[p]
        for first, count in runs:
            final = p == pairs - 1 and first + count == slab
            fields = [taken[s, 0 if s < NEAR else first] for s in range(pen)]
            made = inverse_planes(
                pair_index, p, fields, orbitals, cols_back, depth_back, first, terms, part.shape[1] if final else 0
            )
            terms = made[0]
    return made[1], terms


def pair_fields_plain(orbitals, pair_index, pen):
    slab = NG // pen
    plane_rows = orbitals.shape[1]
    positions = jnp.arange(NG, dtype=jnp.int32)
    places = np.arange(NG)
    high, low = (jnp.asarray(part) for part in split_table(cas_table(places[:, None], places[None, :])))

    def transform(axes, field):
        first = lax.reduce_precision(field, 8, 7)
        second = (field - first).astype(jnp.bfloat16)
        first = first.astype(jnp.bfloat16)
        return (
            jnp.einsum(axes, first, high, preferred_element_type=jnp.float32)
            + jnp.einsum(axes, first, low, preferred_element_type=jnp.float32)
            + jnp.einsum(axes, second, high, preferred_element_type=jnp.float32)
        )

    grid = orbitals.reshape(orbitals.shape[0], plane_rows, NG, NG)
    right = grid[pair_index[:, 1]].astype(jnp.float32)
    field = grid[pair_index[:, 0]].astype(jnp.float32) * right
    field = transform("pxyk,yv->pxvk", transform("pxyz,zk->pxyk", field))
    field = lax.all_to_all(field.astype(jnp.bfloat16), "pen", split_axis=2, concat_axis=1, tiled=True)
    col = signed_freq(lax.axis_index("pen") * slab + jnp.arange(slab, dtype=jnp.int32), NG)
    freq = signed_freq(positions, NG)
    square_sum = (freq * freq)[:, None, None] + (col * col)[None, :, None] + (freq * freq)[None, None, :]
    weights = coulomb_kernel(square_sum, NG) / float(NG * NG * NG)
    field = transform("pxyk,xv->pvyk", field.astype(jnp.float32)) * weights[None]
    field = transform("pxyk,xv->pvyk", field).astype(jnp.bfloat16)
    field = lax.all_to_all(field, "pen", split_axis=1, concat_axis=2, tiled=True)
    field = transform("pxyk,yv->pxvk", field.astype(jnp.float32))
    terms = transform("pxyk,kz->pxyz", field) * right
    return terms.reshape(terms.shape[0], plane_rows, NG * NG)


def tile_pass(tile_blocks, aux_local, pair_ids, live_count, contribute, initial):
    step_rows = 8

    def add_block(step_index, running):
        first_slot = step_index * step_rows
        tile_block = lax.dynamic_slice_in_dim(tile_blocks, first_slot, step_rows, 0)
        aux_block = lax.dynamic_slice_in_dim(aux_local, first_slot, step_rows, 0)
        pair_block = lax.dynamic_slice_in_dim(pair_ids, first_slot, step_rows, 0)
        slot_ids = first_slot + jnp.arange(step_rows, dtype=jnp.int32)
        live_mask = (slot_ids < live_count).astype(jnp.float32)
        return contribute(running, tile_block, aux_block, pair_block, live_mask)

    block_count = (live_count + step_rows - 1) // step_rows
    return lax.fori_loop(0, block_count, add_block, initial)


def to_all(values, count, axes):
    copies = jnp.broadcast_to(values[None], (count, *values.shape))
    return lax.all_to_all(copies, axes, split_axis=0, concat_axis=0, tiled=True)


def coulomb_partial(tile_blocks, tile_aux, tile_pair, tile_count, density, metric_inv):
    aux_count = metric_inv.shape[0]
    dens_all = lax.all_gather(density, "blk", axis=0, tiled=True)
    aux_local = tile_aux - lax.axis_index("pen") * aux_count
    live_count = tile_count[0]
    aux_ids = jnp.arange(aux_count, dtype=jnp.int32)

    def add_fit(running, tile_block, aux_block, pair_block, live_mask):
        dens_rows = dens_all[pair_block]
        partial_value = jnp.einsum("tap,tp->ta", tile_block, dens_rows, preferred_element_type=jnp.float32)
        partial_value = partial_value * live_mask[:, None]
        selector = (aux_block[:, None] == aux_ids[None, :]).astype(jnp.float32)
        return running + jnp.einsum("tk,ta->ka", selector, partial_value, precision=PRECISE)

    gamma = jnp.zeros((aux_count, tile_blocks.shape[1]), jnp.float32)
    gamma = tile_pass(tile_blocks, aux_local, tile_pair, live_count, add_fit, gamma)
    gamma_all = lax.psum(gamma, ("grp", "blk"))
    coef = jnp.einsum("kab,kb->ka", metric_inv, gamma_all, precision=PRECISE).astype(jnp.bfloat16)

    def add_coulomb(running, tile_block, aux_block, pair_block, live_mask):
        selector = (aux_block[:, None] == aux_ids[None, :]).astype(jnp.bfloat16)
        coef_rows = jnp.dot(selector, coef, preferred_element_type=jnp.float32).astype(jnp.bfloat16)
        partial_value = jnp.einsum("tap,ta->tp", tile_block, coef_rows, preferred_element_type=jnp.float32)
        partial_value = partial_value * live_mask[:, None]
        return running.at[pair_block].add(partial_value)

    part = jnp.zeros((dens_all.shape[0], tile_blocks.shape[2]), jnp.float32)
    return tile_pass(tile_blocks, aux_local, tile_pair, live_count, add_coulomb, part)


def body(tile_blocks, tile_aux, tile_pair, tile_count, density, metric_inv, orbitals, pair_index):
    pen, blk, grp = (lax.axis_size(name) for name in ("pen", "blk", "grp"))
    slab = orbitals.shape[1]
    rows = density.shape[0] // (grp * pen)
    tiles = (tile_blocks, tile_aux, tile_pair, tile_count)
    if slab % ROWS == 0 and pen & (pen - 1) == 0 and pen >= NEAR and rows <= ROWS // 3:

        def coulomb_local(after):
            late_density, _ = lax.optimization_barrier((density, after))
            dens_all = to_all(late_density, blk, "blk").reshape(-1, LANE)
            scratch = [pltpu.VMEM(dens_all.shape, jnp.float32)]
            gamma = tile_call(fit_kernel, tiles, dens_all, metric_inv.shape[0], scratch, "fit_tiles")
            gamma = to_all(gamma, grp * blk, ("grp", "blk")).sum(axis=0)
            coef = jnp.einsum("kab,kb->ka", metric_inv, gamma, precision=PRECISE)
            coef = lax.reduce_precision(coef, 8, 7)
            return tile_call(build_kernel, tiles, coef, dens_all.shape[0], [], "build_tiles")

        def coulomb_part(local):
            shares = local.reshape(grp, pen, blk, rows, LANE).transpose(0, 2, 1, 3, 4)
            shares = shares.reshape(grp * blk, pen * rows, LANE)
            taken = lax.all_to_all(shares, ("grp", "blk"), split_axis=0, concat_axis=0, tiled=True)
            return taken.sum(axis=0).reshape(pen, rows, LANE)

        return both_parts(orbitals, pair_index, pen, coulomb_local, coulomb_part)
    part = coulomb_partial(*tiles, density, metric_inv)
    coulomb = lax.psum_scatter(part, ("grp", "pen", "blk"), scatter_dimension=0, tiled=True)
    return coulomb, pair_fields_plain(orbitals, pair_index, pen)


def solution(mesh):
    placed = (
        P(("grp", "pen", "blk"), None, None),
        P(("grp", "pen", "blk")),
        P(("grp", "pen", "blk")),
        P(("grp", "pen", "blk")),
        P("blk", None),
        P("pen", None, None),
        P(None, "pen", None),
        P(("grp", "blk"), None),
    )
    return jax.shard_map(
        body,
        mesh=mesh,
        in_specs=placed,
        out_specs=(P(("grp", "pen", "blk"), None), P(("grp", "blk"), "pen", None)),
        check_vma=False,
    )
```
